512 devices in a mesh: group: 16 (over y, core), dev: 32 (over z, x).
Axes of the slice: x: 4, y: 8, z: 8, core: 2. Of those that a mesh axis runs over, the one named last changes fastest.
Arguments:
- queries: bfloat16 [4096, 2, 8192], P(('group', 'dev')), may hold values from -50 to 50
- new_keys: bfloat16 [4096, 2, 1024], P(('group', 'dev')), may hold values from -6 to 6
- new_values: bfloat16 [4096, 2, 1024], P(('group', 'dev')), may hold values from -24 to 24
- suffix_keys: bfloat16 [4096, 32, 1024], P(('group', 'dev')), may hold values from -6 to 6
- suffix_values: bfloat16 [4096, 32, 1024], P(('group', 'dev')), may hold values from -24 to 24
- suffix_lengths: int32 [4096], P(('group', 'dev')), may hold values from 1 to 32
- root_keys: bfloat16 [1024, 1024], P('group'), may hold values from -6 to 6
- root_values: bfloat16 [1024, 1024], P('group'), may hold values from -24 to 24
- prefix_keys: bfloat16 [1024, 256, 1024], P(('group', 'dev')), may hold values from -6 to 6
- prefix_values: bfloat16 [1024, 256, 1024], P(('group', 'dev')), may hold values from -24 to 24
- prefix_lengths: int32 [1024], P(('group', 'dev')), may hold values from 2 to 256
- owner_map: int32 [16, 64], P('group'), may hold values from 0 to 63, as said below
- block_lists: int32 [4096, 2], P(('group', 'dev')), may hold values from 0 to 63, as said below
Outputs:
- attended: bfloat16 [4096, 2, 8192], P(('group', 'dev'))
The draws below stay inside these ranges and needn't reach their ends.
Inputs may be any that keep to these rules, and one draw needn't show every extreme that they name: Each row is a permutation of 0 to 63: block b of group g is kept by the device owner_map[g, b] // 2 of that group along dev, in its local slot owner_map[g, b] % 2. `block_lists`: block ids of the request's own group; the 2 blocks of one request are distinct. Of the 16 blocks named in one device's rows, at most 2 are kept by any one device, and in every group some device keeps exactly 2 of those of every device of the group.
All inputs are finite; a program needn't handle non-finite values.
Results may differ from the reference program's by a relative error of at most 0.0075.
Values may be sent and summed in bfloat16 or wider, within the bound.
A program may use at most 64 MiB of HBM per device.

```python
import math
import jax
import jax.numpy as jnp
from jax import lax

HEADS = 64
KV_HEADS = 8
HEAD = 128
REQ_DEV = 8
SUF = 32
PB_DEV = 2
BLK = 256
REFS = 2
REQUESTS = 4096
NBLK = 64
BLOCKS = 1024
ROOT = 1024
CAP = 2
N_GROUP = 16
N_DEV = 32
DEVICES = 512


def route_tables(key):
    key = jax.random.fold_in(key, 202)
    key_perm, key_hot, key_pool, key_slot = jax.random.split(key, 4)
    group_keys = jax.random.split(key_perm, N_GROUP)
    owner_table = jax.vmap(lambda member: jax.random.permutation(member, NBLK))(group_keys).astype(jnp.int32)
    inverse = jnp.argsort(owner_table, axis=1).astype(jnp.int32)
    hottest = jax.random.randint(key_hot, (N_GROUP,), 0, N_DEV).astype(jnp.int32)
    pair_count = REQ_DEV * REFS
    source_keys = jax.random.split(key_pool, DEVICES)

    def one_source(source_key, hot_owner):
        first_key, second_key = jax.random.split(source_key)
        others = ((hot_owner + 1 + jnp.arange(N_DEV - 1, dtype=jnp.int32)) % N_DEV).astype(jnp.int32)
        shuffled = jax.random.permutation(first_key, jnp.tile(others, CAP))[:pair_count - CAP]
        targets = jnp.concatenate([jnp.full((CAP,), hot_owner, jnp.int32), shuffled.astype(jnp.int32)])
        return jax.random.permutation(second_key, targets)
    targets = jax.vmap(one_source)(source_keys, jnp.repeat(hottest, N_DEV)).reshape(REQUESTS, REFS)
    offsets = jax.random.randint(key_slot, (REQUESTS, 1), 0, PB_DEV).astype(jnp.int32)
    slot_in = (jnp.arange(REFS, dtype=jnp.int32)[None, :] + offsets) % PB_DEV
    stored = targets * PB_DEV + slot_in
    group_of = jnp.arange(REQUESTS, dtype=jnp.int32) // (REQ_DEV * N_DEV)
    block_table = inverse[group_of[:, None], stored]
    return (owner_table, block_table.astype(jnp.int32))


def draw_owner_map(key, part):
    tables = route_tables(key)
    return tables[0]


def draw_block_lists(key, part):
    tables = route_tables(key)
    return tables[1]


def draw_queries(key, part):
    key = jax.random.fold_in(key, 3)
    shape = (REQUESTS, 2, HEADS * HEAD)
    drawn = 1.5 * jnp.clip(jax.random.normal(key, shape, jnp.float32), -4.0, 4.0)
    return drawn.astype(jnp.bfloat16)


def draw_root_keys(key, part):
    key = jax.random.fold_in(key, 4)
    shape = (ROOT, KV_HEADS * HEAD)
    drawn = jnp.clip(jax.random.normal(key, shape, jnp.float32), -6.0, 6.0)
    return drawn.astype(jnp.bfloat16)


def draw_prefix_keys(key, part):
    key = jax.random.fold_in(key, 5)
    shape = (BLOCKS, BLK, KV_HEADS * HEAD)
    drawn = jnp.clip(jax.random.normal(key, shape, jnp.float32), -6.0, 6.0)
    return drawn.astype(jnp.bfloat16)


def draw_prefix_lengths(key, part):
    key = jax.random.fold_in(key, 6)
    first_key, second_key = jax.random.split(key)
    lengths = jax.random.randint(first_key, (BLOCKS,), 2, BLK + 1)
    spot = jax.random.randint(second_key, (), 0, BLOCKS)
    return jnp.where(jnp.arange(BLOCKS) == spot, BLK, lengths).astype(jnp.int32)


def draw_suffix_lengths(key, part):
    key = jax.random.fold_in(key, 7)
    first_key, second_key = jax.random.split(key)
    lengths = jax.random.randint(first_key, (REQUESTS,), 1, SUF + 1)
    spot = jax.random.randint(second_key, (), 0, REQUESTS)
    return jnp.where(jnp.arange(REQUESTS) == spot, SUF, lengths).astype(jnp.int32)


def block_levels(key, shape, shards, smallest, high):
    loudness, own = 1.0, jax.random.fold_in(key, 6)
    for axis_at, blocks in shards:
        steps = jnp.exp(jax.random.uniform(jax.random.fold_in(own, axis_at), (blocks,), jnp.float32, smallest / len(shards), high / len(shards)))
        loudness = loudness * jnp.repeat(steps, shape[axis_at] // blocks).reshape([-1 if axis == axis_at else 1 for axis in range(len(shape))])
    return loudness


def scatter_about(own_key, dims, deviation, limit, cuts=(), held_as=jnp.bfloat16):
    gain = block_levels(own_key, dims, cuts, -0.22, 0.18) if cuts else 1.0
    values = jax.random.normal(own_key, dims, jnp.float32) * deviation * gain
    return jnp.minimum(jnp.maximum(values, -limit), limit).astype(held_as)


def setup_inputs(seed: int = 0) -> dict:
    key_of = jax.random.split(jax.random.key(seed), 14)
    queries = draw_queries(jax.random.fold_in(key_of[13], 71), 0)
    new_keys = scatter_about(key_of[1], (REQUESTS, 2, KV_HEADS * HEAD), 1.0, 6.0, ((0, 512),))
    new_values = scatter_about(key_of[2], (REQUESTS, 2, KV_HEADS * HEAD), 4.0, 24.0, ((0, 512),))
    suffix_keys = scatter_about(key_of[3], (REQUESTS, SUF, KV_HEADS * HEAD), 1.0, 6.0, ((0, 512),))
    suffix_values = scatter_about(key_of[4], (REQUESTS, SUF, KV_HEADS * HEAD), 4.0, 24.0, ((0, 512),))
    suffix_lengths = draw_suffix_lengths(jax.random.fold_in(key_of[13], 71), 0)
    root_keys = draw_root_keys(jax.random.fold_in(key_of[13], 71), 0)
    root_values = scatter_about(key_of[7], (ROOT, KV_HEADS * HEAD), 4.0, 24.0, ((0, 16),))
    prefix_keys = draw_prefix_keys(jax.random.fold_in(key_of[13], 71), 0)
    prefix_values = scatter_about(key_of[9], (BLOCKS, BLK, KV_HEADS * HEAD), 4.0, 24.0, ((0, 512),))
    prefix_lengths = draw_prefix_lengths(jax.random.fold_in(key_of[13], 71), 0)
    owner_map = draw_owner_map(jax.random.fold_in(key_of[13], 71), 0)
    block_lists = draw_block_lists(jax.random.fold_in(key_of[13], 71), 0)
    return dict(queries=queries, new_keys=new_keys, new_values=new_values, suffix_keys=suffix_keys, suffix_values=suffix_values, suffix_lengths=suffix_lengths, root_keys=root_keys, root_values=root_values, prefix_keys=prefix_keys, prefix_values=prefix_values, prefix_lengths=prefix_lengths, owner_map=owner_map, block_lists=block_lists)


def rounded_weights(weights):
    return lax.optimization_barrier(weights.astype(jnp.bfloat16)).astype(jnp.float32)

def reference(queries, new_keys, new_values, suffix_keys, suffix_values, suffix_lengths, root_keys, root_values, prefix_keys, prefix_values, prefix_lengths, owner_map, block_lists):
    per_kv = HEADS // KV_HEADS
    score_scale = 1.0 / math.sqrt(HEAD)
    block_rows = 16
    block_count = REQUESTS // block_rows
    root_key_f = root_keys.astype(jnp.float32).reshape(ROOT, KV_HEADS, HEAD)
    root_value_f = root_values.astype(jnp.float32).reshape(ROOT, KV_HEADS, HEAD)
    request_rows = jnp.arange(REQUESTS, dtype=jnp.int32)

    def one_block(operands):
        query_rows, fresh_keys, fresh_values, past_keys, past_values, past_lengths, blocks, row_ids = operands
        row_count = query_rows.shape[0]
        heads_q = query_rows.astype(jnp.float32).reshape(row_count, 2, KV_HEADS, per_kv, HEAD)
        root_scores = jnp.einsum('rtkgd,lkd->rtkgl', heads_q, root_key_f) * score_scale
        past_k = past_keys.astype(jnp.float32).reshape(row_count, SUF, KV_HEADS, HEAD)
        past_v = past_values.astype(jnp.float32).reshape(row_count, SUF, KV_HEADS, HEAD)
        past_scores = jnp.einsum('rtkgd,rlkd->rtkgl', heads_q, past_k) * score_scale
        past_valid = jnp.arange(SUF, dtype=jnp.int32)[None, :] < past_lengths[:, None]
        past_scores = jnp.where(past_valid[:, None, None, None, :], past_scores, -jnp.inf)
        fresh_k = fresh_keys.astype(jnp.float32).reshape(row_count, 2, KV_HEADS, HEAD)
        fresh_v = fresh_values.astype(jnp.float32).reshape(row_count, 2, KV_HEADS, HEAD)
        fresh_scores = jnp.einsum('rtkgd,rjkd->rtkgj', heads_q, fresh_k) * score_scale
        fresh_valid = jnp.arange(2, dtype=jnp.int32)[None, :] <= jnp.arange(2, dtype=jnp.int32)[:, None]
        fresh_scores = jnp.where(fresh_valid[None, :, None, None, :], fresh_scores, -jnp.inf)
        scores = jnp.concatenate([root_scores, past_scores, fresh_scores], axis=-1)
        highest = lax.optimization_barrier(jnp.max(scores, axis=-1))
        weights = jnp.exp(scores - highest[..., None])
        totals = lax.optimization_barrier(jnp.sum(weights, axis=-1))
        rounded = rounded_weights(weights)
        summed = jnp.einsum('rtkgl,lkd->rtkgd', rounded[..., :ROOT], root_value_f)
        summed = summed + jnp.einsum('rtkgl,rlkd->rtkgd', rounded[..., ROOT:ROOT + SUF], past_v)
        summed = summed + jnp.einsum('rtkgl,rlkd->rtkgd', rounded[..., ROOT + SUF:], fresh_v)
        group_of = (row_ids // (REQ_DEV * N_DEV)).astype(jnp.int32)
        largest = highest
        pieces_out = []
        for ref_index in range(REFS):
            stored = (group_of * NBLK + owner_map[group_of, blocks[:, ref_index]]).astype(jnp.int32)
            block_k = prefix_keys[stored].astype(jnp.float32).reshape(row_count, BLK, KV_HEADS, HEAD)
            block_v = prefix_values[stored].astype(jnp.float32).reshape(row_count, BLK, KV_HEADS, HEAD)
            part_scores = jnp.einsum('rtkgd,rlkd->rtkgl', heads_q, block_k) * score_scale
            block_valid = jnp.arange(BLK, dtype=jnp.int32)[None, :] < prefix_lengths[stored][:, None]
            part_scores = jnp.where(block_valid[:, None, None, None, :], part_scores, -jnp.inf)
            part_highest = lax.optimization_barrier(jnp.max(part_scores, axis=-1))
            part_weights = jnp.exp(part_scores - part_highest[..., None])
            part_totals = lax.optimization_barrier(jnp.sum(part_weights, axis=-1))
            part_summed = jnp.einsum('rtkgl,rlkd->rtkgd', rounded_weights(part_weights), block_v)
            answer = rounded_weights(part_summed / part_totals[..., None])
            log_total = part_highest + jnp.log(part_totals)
            pieces_out.append((answer, log_total))
            largest = jnp.maximum(largest, log_total)
        numerator = summed * jnp.exp(highest - largest)[..., None]
        denominator = totals * jnp.exp(highest - largest)
        for answer, log_total in pieces_out:
            weight_of = jnp.exp(log_total - largest)
            numerator = numerator + weight_of[..., None] * answer
            denominator = denominator + weight_of
        return (numerator / denominator[..., None]).reshape(row_count, 2, HEADS * HEAD).astype(jnp.bfloat16)
    operands = (queries.reshape(block_count, block_rows, 2, HEADS * HEAD), new_keys.reshape(block_count, block_rows, 2, KV_HEADS * HEAD), new_values.reshape(block_count, block_rows, 2, KV_HEADS * HEAD), suffix_keys.reshape(block_count, block_rows, SUF, KV_HEADS * HEAD), suffix_values.reshape(block_count, block_rows, SUF, KV_HEADS * HEAD), suffix_lengths.reshape(block_count, block_rows), block_lists.reshape(block_count, block_rows, REFS), request_rows.reshape(block_count, block_rows))
    result = lax.map(one_block, operands)
    return result.reshape(REQUESTS, 2, HEADS * HEAD)
```

```python
import functools
import math

import jax
import jax.numpy as jnp
from jax import lax
from jax.experimental import pallas as pl
from jax.experimental.pallas import tpu as pltpu
from jax.sharding import PartitionSpec as P

KV = 8
HEAD = 128
NX = 4
CORES = 2
REQ = 8
ROWS = 128
SLOT_ROWS = 32
BLK = 256
SUF = 32
LOCAL = 384
HALF = KV // 2
FLOOR = -1.0e30
DROP = -2.0e30
SCALE = 1.0 / math.sqrt(HEAD)
SCALE2 = SCALE / math.log(2.0)
MESH = pl.DeviceIdType.MESH
NT = (((1,), (1,)), ((), ()))


def iota(shape, dim):
    return lax.broadcasted_iota(jnp.int32, shape, dim)


def kernel(
    nz,
    ny,
    q_ref,
    nk_ref,
    nv_ref,
    sk_ref,
    sv_ref,
    rk_ref,
    rv_ref,
    pk_ref,
    pv_ref,
    slen_ref,
    plen_ref,
    om_ref,
    bl_ref,
    out_ref,
    zq,
    snd,
    rcv,
    ans,
    ret,
    rsin,
    rsout,
    rkv,
    pk,
    pv,
    sk,
    sv,
    metaz,
    metax,
    onehot,
    bias_t,
    pick,
    kbias,
    lbias,
    lpick,
    lmine,
    lret,
    lslot,
    lin,
    lout,
    loc_acc,
    loc_max,
    loc_tot,
    lacc,
    local_sem,
    zs_sem,
    zr_sem,
    ms_sem,
    mr_sem,
    nsend_sem,
    nrecv_sem,
    xs_sem,
    xr_sem,
    bs_sem,
    br_sem,
    ls_sem,
    lr_sem,
    rs_sem,
    rr_sem,
    es_sem,
    er_sem,
    ys_sem,
    yr_sem,
    cs_sem,
    cr_sem,
):
    zh = nz // 2
    yh = ny // 2
    group = lax.axis_index("group")
    dev = lax.axis_index("dev")
    z, x = dev // NX, dev % NX
    y, core = group // CORES, group % CORES

    def at_z(step):
        return (group, lax.rem(z + step + nz, nz) * NX + x)

    def at_x(step):
        return (group, z * NX + lax.rem(x + step, NX))

    def at_y(step):
        return (lax.rem(y + step + ny, ny) * CORES + core, dev)

    sibling = (y * CORES + 1 - core, dev)
    drains = []

    def send(src, dst, send_sem, recv_sem, device):
        copy = pltpu.make_async_remote_copy(
            src_ref=src,
            dst_ref=dst,
            send_sem=send_sem,
            recv_sem=recv_sem,
            device_id=device,
            device_id_type=MESH,
        )
        copy.start()
        drains.append(copy)

    def arrived(ref, send_sem, recv_sem, device):
        pltpu.make_async_remote_copy(
            src_ref=ref,
            dst_ref=ref,
            send_sem=send_sem,
            recv_sem=recv_sem,
            device_id=device,
            device_id_type=MESH,
        ).wait_recv()

    loads = [
        pltpu.make_async_copy(rk_ref, rkv.at[0, 0], local_sem.at[0]),
        pltpu.make_async_copy(rv_ref, rkv.at[0, 1], local_sem.at[1]),
        pltpu.make_async_copy(pk_ref, pk, local_sem.at[2]),
        pltpu.make_async_copy(pv_ref, pv, local_sem.at[3]),
        pltpu.make_async_copy(sk_ref, sk.at[pl.ds(0, REQ * SUF)], local_sem.at[4]),
        pltpu.make_async_copy(sv_ref, sv.at[pl.ds(0, REQ * SUF)], local_sem.at[5]),
    ]
    for load in loads:
        load.start()

    partners = [at_z(step) for step in range(1, nz)]
    partners += [at_x(step) for step in range(1, NX)]
    if ny > 1:
        partners += [at_y(1), at_y(-1)]
    partners += [sibling]
    barrier = pltpu.get_barrier_semaphore()
    for partner in partners:
        pl.semaphore_signal(barrier, inc=1, device_id=partner, device_id_type=MESH)

    lane1 = iota((1, ROWS), 1)
    stored = [om_ref[0, bl_ref[p // 2, p % 2]] for p in range(2 * REQ)]
    owner = [s // 2 for s in stored]
    code_rows = [jnp.zeros((1, ROWS), jnp.int32), jnp.zeros((1, ROWS), jnp.int32)]
    for p in range(2 * REQ):
        rank = jnp.int32(0)
        for other in range(p):
            rank = rank + (owner[other] == owner[p]).astype(jnp.int32)
        code = owner[p] * 4 + rank * 2 + stored[p] % 2
        code_rows[p % 2] = jnp.where(lane1 // 16 == p // 2, code, code_rows[p % 2])
    metaz[0, pl.ds(0, 1), :] = code_rows[0]
    metaz[0, pl.ds(1, 1), :] = code_rows[1]

    pl.semaphore_wait(barrier, len(partners))

    def q_half(b, h):
        rows = pl.ds(h * HALF, HALF)
        return q_ref.at[rows] if b == 0 else zq.at[b, rows]

    def pass_queries(b, h, step, into):
        send(
            q_half(b, h),
            zq.at[into, pl.ds(h * HALF, HALF)],
            zs_sem.at[into, h],
            zr_sem.at[into, h],
            at_z(step),
        )

    def forward_queries(b, h):
        for step in (1, -1):
            if b == 0 or (step == 1) == (b > zh):
                if b == zh:
                    continue
                into = (b - step) % nz
                if into == zh and h != (0 if step == 1 else 1):
                    continue
                pass_queries(b, h, step, into)

    def query_arrived(b, h):
        arrived(
            zq.at[b, pl.ds(h * HALF, HALF)], zs_sem.at[b, h], zr_sem.at[b, h], at_z(1)
        )

    for h in range(2):
        forward_queries(0, h)
    for step in range(1, nz):
        send(
            metaz.at[0],
            metaz.at[(-step) % nz],
            ms_sem.at[step],
            mr_sem.at[(-step) % nz],
            at_z(step),
        )

    loads[0].wait()
    loads[1].wait()

    def share_root(b):
        send(rkv.at[b], rkv.at[ny + b], cs_sem.at[b], cr_sem.at[b], sibling)

    def forward_root(b):
        for step in (1, -1):
            if b == 0 or (step == 1) == (b > yh):
                if b == yh or ny == 1:
                    continue
                into = (b - step) % ny
                if into == yh:
                    part = 0 if step == 1 else 1
                    send(
                        rkv.at[b, part],
                        rkv.at[into, part],
                        ys_sem.at[into, part],
                        yr_sem.at[into, part],
                        at_y(step),
                    )
                else:
                    send(
                        rkv.at[b],
                        rkv.at[into],
                        ys_sem.at[into, 0],
                        yr_sem.at[into, 0],
                        at_y(step),
                    )

    def root_arrived(b):
        if b == yh:
            for part in range(2):
                arrived(rkv.at[b, part], ys_sem.at[b, part], yr_sem.at[b, part], at_y(1))
        else:
            arrived(rkv.at[b], ys_sem.at[b, 0], yr_sem.at[b, 0], at_y(1))

    forward_root(0)
    share_root(0)

    row = iota((ROWS, ROWS), 0)
    lane = iota((ROWS, ROWS), 1)
    same_place = row % 16 == lane % 16
    diagonal = jnp.where(row == lane, 0.0, DROP)

    def select(b):
        wanted = z * (2 * NX) + row // 16
        first = metaz[b, pl.ds(0, 1), :] // 2
        second = metaz[b, pl.ds(1, 1), :] // 2
        hit = ((first == wanted) | (second == wanted)) & same_place
        onehot[b] = jnp.where(hit, 1.0, 0.0).astype(jnp.bfloat16)
        bias_t[b] = jnp.where(hit, 0.0, DROP).T
        mine = pl.ds(pl.multiple_of(x * SLOT_ROWS, SLOT_ROWS), SLOT_ROWS)

        def body(k, carry):
            block = q_ref[k] if b == 0 else zq[b, k]
            chosen = jnp.dot(onehot[b], block, preferred_element_type=jnp.float32)
            snd[b, k] = chosen.astype(jnp.bfloat16)
            rcv[b, k, mine, :] = snd[b, k, mine, :]
            return carry

        lax.fori_loop(0, KV, body, 0)
        for step in range(1, NX):
            there = pl.ds(pl.multiple_of(lax.rem(x + step, NX) * SLOT_ROWS, SLOT_ROWS), SLOT_ROWS)
            send(
                snd.at[b, :, there, :],
                rcv.at[b, :, mine, :],
                xs_sem.at[b, NX - step],
                xr_sem.at[b, NX - step],
                at_x(step),
            )

    def slots_arrived(b):
        for step in range(1, NX):
            there = pl.ds(pl.multiple_of(lax.rem(x + step, NX) * SLOT_ROWS, SLOT_ROWS), SLOT_ROWS)
            arrived(
                rcv.at[b, :, there, :], xs_sem.at[b, step], xr_sem.at[b, step], at_x(step)
            )

    ones_prefix = jnp.ones((2 * BLK, HEAD), jnp.bfloat16)

    def serve(b):
        slots_arrived(b)
        for source in range(NX):
            code = metax[source, b]
            srow = iota((SLOT_ROWS, ROWS), 0)
            slane = iota((SLOT_ROWS, ROWS), 1)
            wanted = (dev * 2 + srow // 16) * 2 + 1
            hit = (code[0:1, :] == wanted) | (code[1:2, :] == wanted)
            second = jnp.max(jnp.where(hit, 1.0, 0.0), axis=1, keepdims=True)
            pick[b, pl.ds(source * SLOT_ROWS, SLOT_ROWS), :] = jnp.where(
                slane == 0, 1.0 - second, jnp.where(slane == 1, second, 0.0)
            ).astype(jnp.bfloat16)

        def body(k, carry):
            cols = pl.ds(pl.multiple_of(k * HEAD, HEAD), HEAD)
            queries = jnp.concatenate([rcv[b, k], pick[b]], axis=1)
            keys = jnp.concatenate([pk[:, cols], kbias[...]], axis=1)
            scores = lax.dot_general(queries, keys, NT, preferred_element_type=jnp.float32)
            highest = jnp.max(scores, axis=1, keepdims=True)
            weights = jnp.exp2((scores - highest) * SCALE2).astype(jnp.bfloat16)
            values = jnp.concatenate([pv[:, cols], ones_prefix], axis=1)
            summed = jnp.dot(weights, values, preferred_element_type=jnp.float32)
            totals = summed[:, HEAD:]
            ans[b, k] = (summed[:, :HEAD] / totals).astype(jnp.bfloat16)
            lacc[...] = jnp.where(lane == k, highest * SCALE + jnp.log(totals), lacc[...])
            return carry

        lax.fori_loop(0, KV, body, 0)
        lmine[b] = lacc[...].T[:KV, :]

    def give_back(b):
        mine = pl.ds(pl.multiple_of(x * SLOT_ROWS, SLOT_ROWS), SLOT_ROWS)
        for step in range(1, NX):
            there = pl.ds(pl.multiple_of(lax.rem(x + step, NX) * SLOT_ROWS, SLOT_ROWS), SLOT_ROWS)
            send(
                ans.at[b, :, there, :],
                ret.at[b, :, mine, :],
                bs_sem.at[b, NX - step],
                br_sem.at[b, NX - step],
                at_x(step),
            )
            send(
                lmine.at[b],
                lret.at[b, NX - step],
                ls_sem.at[b, NX - step],
                lr_sem.at[b, NX - step],
                at_x(step),
            )

        def body(k, carry):
            ret[b, k, mine, :] = ans[b, k, mine, :]
            return carry

        lax.fori_loop(0, KV, body, 0)

    def answers_arrived(b):
        lane8 = iota((KV, ROWS), 1)
        rows = lmine[b]
        for step in range(1, NX):
            there = pl.ds(pl.multiple_of(lax.rem(x + step, NX) * SLOT_ROWS, SLOT_ROWS), SLOT_ROWS)
            arrived(
                ret.at[b, :, there, :], bs_sem.at[b, step], br_sem.at[b, step], at_x(step)
            )
            arrived(lret.at[b, step], ls_sem.at[b, step], lr_sem.at[b, step], at_x(step))
            moved = pltpu.roll(lret[b, step], SLOT_ROWS * step, 1)
            rows = jnp.where(lane8 // SLOT_ROWS == lax.rem(x + step, NX), moved, rows)
        lslot[b] = rows

    def chain(b, h):
        step = 1 if b < zh or (b == zh and h == 0) else -1
        into = (b - step) % nz
        place = into if into else (0 if step == 1 else zh)
        return step, place

    def has_input(b, h):
        return b != zh and (b not in (zh - 1, zh + 1) or chain(zh, h)[1] == b)

    def partial_arrived(place, h):
        arrived(
            rsin.at[place, pl.ds(h * HALF, HALF)],
            rs_sem.at[place, h],
            rr_sem.at[place, h],
            at_z(1),
        )
        arrived(lin.at[place, h], es_sem.at[place, h], er_sem.at[place, h], at_z(1))

    def combine(b, h):
        fed = has_input(b, h)
        if fed:
            partial_arrived(b, h)

        def body(k, carry):
            rows = jnp.broadcast_to(lslot[b, pl.ds(k, 1), :], (ROWS, ROWS)) + bias_t[b]
            parts = ret[b, k]
            if fed:
                extra = jnp.broadcast_to(lin[b, h, pl.ds(k, 1), :], (ROWS, ROWS)) + diagonal
                rows = jnp.concatenate([rows, extra], axis=1)
                parts = jnp.concatenate([parts, rsin[b, k]], axis=0)
            highest = jnp.maximum(jnp.max(rows, axis=1, keepdims=True), FLOOR)
            weights = jnp.exp(rows - highest).astype(jnp.bfloat16)
            parts = jnp.concatenate([parts, jnp.ones_like(parts)], axis=1)
            summed = jnp.dot(weights, parts, preferred_element_type=jnp.float32)
            totals = jnp.maximum(summed[:, HEAD:], 1.0e-30)
            rsout[b, k] = (summed[:, :HEAD] / totals).astype(jnp.bfloat16)
            lacc[...] = jnp.where(lane == k, highest + jnp.log(totals), lacc[...])
            return carry

        lax.fori_loop(h * HALF, (h + 1) * HALF, body, 0)
        lout[b, h] = lacc[...].T[:KV, :]
        step, place = chain(b, h)
        part = pl.ds(h * HALF, HALF)
        send(
            rsout.at[b, part],
            rsin.at[place, part],
            rs_sem.at[place, h],
            rr_sem.at[place, h],
            at_z(step),
        )
        send(
            lout.at[b, h],
            lin.at[place, h],
            es_sem.at[place, h],
            er_sem.at[place, h],
            at_z(step),
        )

    ones_root = jnp.ones((ny * CORES * rkv.shape[2], HEAD), jnp.bfloat16)
    ones_local = jnp.ones((LOCAL, HEAD), jnp.bfloat16)
    root_rows = ny * CORES * rkv.shape[2]

    def attend_local(k_from, k_to):
        def body(k, carry):
            cols = pl.ds(pl.multiple_of(k * HEAD, HEAD), HEAD)
            queries = q_ref[k]
            root_keys = rkv[:, 0, :, cols].reshape(root_rows, HEAD)
            root_values = rkv[:, 1, :, cols].reshape(root_rows, HEAD)
            root_scores = lax.dot_general(
                queries, root_keys, NT, preferred_element_type=jnp.float32
            )
            wide = jnp.concatenate([queries, lpick[...]], axis=1)
            keys = jnp.concatenate([sk[:, cols], lbias[...]], axis=1)
            scores = lax.dot_general(wide, keys, NT, preferred_element_type=jnp.float32)
            highest = jnp.maximum(
                jnp.max(root_scores, axis=1, keepdims=True),
                jnp.max(scores, axis=1, keepdims=True),
            )
            root_weights = jnp.exp2((root_scores - highest) * SCALE2).astype(jnp.bfloat16)
            weights = jnp.exp2((scores - highest) * SCALE2).astype(jnp.bfloat16)
            summed = jnp.dot(
                root_weights,
                jnp.concatenate([root_values, ones_root], axis=1),
                preferred_element_type=jnp.float32,
            ) + jnp.dot(
                weights,
                jnp.concatenate([sv[:, cols], ones_local], axis=1),
                preferred_element_type=jnp.float32,
            )
            loc_acc[k] = summed[:, :HEAD]
            loc_tot[k] = summed[:, HEAD:]
            loc_max[k] = jnp.broadcast_to(highest * SCALE, (ROWS, ROWS))
            return carry

        lax.fori_loop(k_from, k_to, body, 0)

    def finish(h):
        partial_arrived(0, h)
        partial_arrived(zh, h)

        def body(k, carry):
            rows = jnp.concatenate(
                [
                    jnp.broadcast_to(lslot[0, pl.ds(k, 1), :], (ROWS, ROWS)) + bias_t[0],
                    jnp.broadcast_to(lin[0, h, pl.ds(k, 1), :], (ROWS, ROWS)) + diagonal,
                    jnp.broadcast_to(lin[zh, h, pl.ds(k, 1), :], (ROWS, ROWS)) + diagonal,
                ],
                axis=1,
            )
            highest = jnp.maximum(jnp.max(rows, axis=1, keepdims=True), loc_max[k])
            wide = jnp.concatenate([highest] * 3, axis=1)
            weights = jnp.exp(rows - wide).astype(jnp.bfloat16)
            parts = jnp.concatenate([ret[0, k], rsin[0, k], rsin[zh, k]], axis=0)
            parts = jnp.concatenate([parts, jnp.ones_like(parts)], axis=1)
            summed = jnp.dot(weights, parts, preferred_element_type=jnp.float32)
            share = jnp.exp(loc_max[k] - highest)
            numerator = summed[:, :HEAD] + loc_acc[k] * share
            denominator = summed[:, HEAD:] + loc_tot[k] * share
            out_ref[k] = (numerator / denominator).astype(jnp.bfloat16)
            return carry

        lax.fori_loop(h * HALF, (h + 1) * HALF, body, 0)

    lacc[...] = jnp.zeros_like(lacc)
    select(0)

    for b in range(1, nz):
        arrived(metaz.at[b], ms_sem.at[b], mr_sem.at[b], at_z(1))
    for step in range(1, NX):
        send(
            metaz,
            metax.at[x],
            nsend_sem.at[NX - step],
            nrecv_sem.at[NX - step],
            at_x(step),
        )
    metax[x] = metaz[...]

    prow = iota((2 * BLK, HEAD), 0)
    plane = iota((2 * BLK, HEAD), 1)
    limit = jnp.where(prow < BLK, plen_ref[0], plen_ref[1])
    live = prow % BLK < limit
    kbias[...] = jnp.where(
        (plane < 2) & ~((plane == prow // BLK) & live), DROP, 0.0
    ).astype(jnp.bfloat16)
    lrow = iota((LOCAL, HEAD), 0)
    llane = iota((LOCAL, HEAD), 1)
    length = jnp.zeros((LOCAL, HEAD), jnp.int32)
    for r in range(REQ):
        length = jnp.where(lrow // SUF == r, slen_ref[r], length)
    past = (lrow < REQ * SUF) & (llane // 2 == lrow // SUF) & (lrow % SUF < length)
    fresh_row = lrow - REQ * SUF
    fresh = (
        (fresh_row >= 0)
        & (fresh_row < 2 * REQ)
        & (llane // 2 == fresh_row // 2)
        & (fresh_row % 2 <= llane % 2)
    )
    lbias[...] = jnp.where((llane < 2 * REQ) & ~(past | fresh), DROP, 0.0).astype(jnp.bfloat16)
    lpick[...] = jnp.where(lane == row // 8, 1.0, 0.0).astype(jnp.bfloat16)
    blank = jnp.zeros((LOCAL - REQ * SUF - 2 * REQ, KV * HEAD), jnp.bfloat16)
    for cache, new in ((sk, nk_ref), (sv, nv_ref)):
        cache[pl.ds(REQ * SUF, 2 * REQ), :] = new[...]
        cache[pl.ds(REQ * SUF + 2 * REQ, LOCAL - REQ * SUF - 2 * REQ), :] = blank

    for load in loads[2:]:
        load.wait()
    meta_waited = False

    waiting = [0]
    for s in range(1, zh + 1):
        blocks = (nz - s, s) if s < zh else (zh,)
        for h in range(2):
            for b in blocks:
                query_arrived(b, h)
                forward_queries(b, h)
        for b in blocks:
            select(b)
        if s <= yh:
            for b in (ny - s, s) if s < yh else (yh,):
                root_arrived(b)
                forward_root(b)
                share_root(b)
        if not meta_waited:
            meta_waited = True
            for step in range(1, NX):
                arrived(
                    metax.at[lax.rem(x + step, NX)],
                    nsend_sem.at[step],
                    nrecv_sem.at[step],
                    at_x(step),
                )
        for b in waiting:
            serve(b)
        waiting = list(blocks)
    for s in range(zh + 1, yh + 1):
        for b in (ny - s, s) if s < yh else (yh,):
            root_arrived(b)
            forward_root(b)
            share_root(b)

    for b in waiting:
        serve(b)
    give_back(zh)
    order = [(zh,)] + [(s, nz - s) for s in range(zh - 1, 0, -1)] + [(0,)]
    for b in order[1]:
        give_back(b)

    for b in range(ny):
        arrived(rkv.at[ny + b], cs_sem.at[b], cr_sem.at[b], sibling)
    per_turn = -(-KV // zh)
    done = 0
    for turn, blocks in enumerate(order[:-1]):
        for b in blocks:
            answers_arrived(b)
        for h in range(2):
            for b in blocks:
                combine(b, h)
        if turn + 2 < len(order):
            for b in order[turn + 2]:
                give_back(b)
        upto = min(KV, done + per_turn)
        if done < upto:
            attend_local(done, upto)
        done = upto
    answers_arrived(0)
    for h in range(2):
        finish(h)

    for copy in drains:
        copy.wait_send()


def shards(nz, ny, *args):
    (
        queries,
        new_keys,
        new_values,
        suffix_keys,
        suffix_values,
        suffix_lengths,
        root_keys,
        root_values,
        prefix_keys,
        prefix_values,
        prefix_lengths,
        owner_map,
        block_lists,
    ) = args
    width = KV * HEAD
    head_major = (
        queries.reshape(REQ, 2, KV, 8, HEAD).transpose(2, 0, 1, 3, 4).reshape(KV, ROWS, HEAD)
    )
    root_rows = root_keys.shape[0]
    bf16, f32 = jnp.bfloat16, jnp.float32
    vmem = pl.BlockSpec(memory_space=pltpu.VMEM)
    smem = pl.BlockSpec(memory_space=pltpu.SMEM)
    anywhere = pl.BlockSpec(memory_space=pl.ANY)
    dma = pltpu.SemaphoreType.DMA
    blocks = (nz, KV, ROWS, HEAD)
    out = pl.pallas_call(
        functools.partial(kernel, nz, ny),
        out_shape=jax.ShapeDtypeStruct((KV, ROWS, HEAD), bf16),
        in_specs=[vmem, vmem, vmem] + [anywhere] * 6 + [smem] * 4,
        out_specs=vmem,
        scratch_shapes=[
            pltpu.VMEM(blocks, bf16),
            pltpu.VMEM(blocks, bf16),
            pltpu.VMEM(blocks, bf16),
            pltpu.VMEM(blocks, bf16),
            pltpu.VMEM(blocks, bf16),
            pltpu.VMEM(blocks, bf16),
            pltpu.VMEM(blocks, bf16),
            pltpu.VMEM((2 * ny, 2, root_rows, width), bf16),
            pltpu.VMEM((2 * BLK, width), bf16),
            pltpu.VMEM((2 * BLK, width), bf16),
            pltpu.VMEM((LOCAL, width), bf16),
            pltpu.VMEM((LOCAL, width), bf16),
            pltpu.VMEM((nz, 2, ROWS), jnp.int32),
            pltpu.VMEM((NX, nz, 2, ROWS), jnp.int32),
            pltpu.VMEM((nz, ROWS, ROWS), bf16),
            pltpu.VMEM((nz, ROWS, ROWS), f32),
            pltpu.VMEM((nz, ROWS, HEAD), bf16),
            pltpu.VMEM((2 * BLK, HEAD), bf16),
            pltpu.VMEM((LOCAL, HEAD), bf16),
            pltpu.VMEM((ROWS, HEAD), bf16),
            pltpu.VMEM((nz, KV, ROWS), f32),
            pltpu.VMEM((nz, NX, KV, ROWS), f32),
            pltpu.VMEM((nz, KV, ROWS), f32),
            pltpu.VMEM((nz, 2, KV, ROWS), f32),
            pltpu.VMEM((nz, 2, KV, ROWS), f32),
            pltpu.VMEM((KV, ROWS, HEAD), f32),
            pltpu.VMEM((KV, ROWS, HEAD), f32),
            pltpu.VMEM((KV, ROWS, HEAD), f32),
            pltpu.VMEM((ROWS, ROWS), f32),
            dma((6,)),
            dma((nz, 2)),
            dma((nz, 2)),
            dma((nz,)),
            dma((nz,)),
            dma((NX,)),
            dma((NX,)),
            dma((nz, NX)),
            dma((nz, NX)),
            dma((nz, NX)),
            dma((nz, NX)),
            dma((nz, NX)),
            dma((nz, NX)),
            dma((nz, 2)),
            dma((nz, 2)),
            dma((nz, 2)),
            dma((nz, 2)),
            dma((ny, 2)),
            dma((ny, 2)),
            dma((ny,)),
            dma((ny,)),
        ],
        compiler_params=pltpu.CompilerParams(
            collective_id=0, has_side_effects=True, vmem_limit_bytes=48 * 1024 * 1024
        ),
        cost_estimate=pl.CostEstimate(
            flops=4_000_000_000, bytes_accessed=5_000_000, transcendentals=8_000_000
        ),
        name="shared_prefix_attention",
    )(
        head_major,
        new_keys.reshape(2 * REQ, width),
        new_values.reshape(2 * REQ, width),
        suffix_keys.reshape(REQ * SUF, width),
        suffix_values.reshape(REQ * SUF, width),
        root_keys,
        root_values,
        prefix_keys.reshape(2 * BLK, width),
        prefix_values.reshape(2 * BLK, width),
        suffix_lengths,
        prefix_lengths,
        owner_map,
        block_lists,
    )
    return out.reshape(KV, REQ, 2, 8, HEAD).transpose(1, 2, 0, 3, 4).reshape(REQ, 2, 64 * HEAD)


def solution(mesh):
    return jax.shard_map(
        functools.partial(shards, mesh.shape["dev"] // NX, mesh.shape["group"] // CORES),
        mesh=mesh,
        in_specs=(
            P(("group", "dev"), None, None),
            P(("group", "dev"), None, None),
            P(("group", "dev"), None, None),
            P(("group", "dev"), None, None),
            P(("group", "dev"), None, None),
            P(("group", "dev")),
            P("group", None),
            P("group", None),
            P(("group", "dev"), None, None),
            P(("group", "dev"), None, None),
            P(("group", "dev")),
            P("group", None),
            P(("group", "dev"), None),
        ),
        out_specs=P(("group", "dev"), None, None),
        check_vma=False,
    )
```

```python
import functools
import math

import jax
import jax.numpy as jnp
from jax import lax
from jax.experimental import pallas as pl
from jax.experimental.pallas import tpu as pltpu
from jax.sharding import PartitionSpec as P

KV = 8
HEAD = 128
NX = 4
CORES = 2
REQ = 8
ROWS = 128
SLOT_ROWS = 32
BLK = 256
SUF = 32
LOCAL = 384
HALF = KV // 2
FLOOR = -1.0e30
DROP = -2.0e30
SCALE = 1.0 / math.sqrt(HEAD)
LOG2E = 1.0 / math.log(2.0)
SCALE2 = SCALE * LOG2E
MESH = pl.DeviceIdType.MESH
NT = (((1,), (1,)), ((), ()))


def iota(shape, dim):
    return lax.broadcasted_iota(jnp.int32, shape, dim)


def kernel(
    nz,
    ny,
    q_ref,
    nk_ref,
    nv_ref,
    sk_ref,
    sv_ref,
    rk_ref,
    rv_ref,
    pk_ref,
    pv_ref,
    slen_ref,
    plen_ref,
    om_ref,
    bl_ref,
    out_ref,
    zq,
    snd,
    rcv,
    ans,
    ret,
    rsin,
    rsout,
    rkv,
    pk,
    pv,
    sk,
    sv,
    metaz,
    metax,
    onehot,
    bias_t,
    pick,
    kbias,
    lbias,
    lpick,
    lmine,
    lret,
    lslot,
    lin,
    lout,
    loc_acc,
    loc_max,
    loc_tot,
    lacc,
    second_slot,
    local_sem,
    zs_sem,
    zr_sem,
    ms_sem,
    mr_sem,
    nsend_sem,
    nrecv_sem,
    xs_sem,
    xr_sem,
    bs_sem,
    br_sem,
    ls_sem,
    lr_sem,
    rs_sem,
    rr_sem,
    es_sem,
    er_sem,
    ys_sem,
    yr_sem,
    cs_sem,
    cr_sem,
):
    zh = nz // 2
    yh = ny // 2
    group = lax.axis_index("group")
    dev = lax.axis_index("dev")
    z, x = dev // NX, dev % NX
    y, core = group // CORES, group % CORES

    def at_z(step):
        return (group, lax.rem(z + step + nz, nz) * NX + x)

    def at_x(step):
        return (group, z * NX + lax.rem(x + step, NX))

    def at_y(step):
        return (lax.rem(y + step + ny, ny) * CORES + core, dev)

    sibling = (y * CORES + 1 - core, dev)
    drains = []

    def send(src, dst, send_sem, recv_sem, device):
        copy = pltpu.make_async_remote_copy(
            src_ref=src,
            dst_ref=dst,
            send_sem=send_sem,
            recv_sem=recv_sem,
            device_id=device,
            device_id_type=MESH,
        )
        copy.start()
        drains.append(copy)

    def arrived(ref, send_sem, recv_sem, device):
        pltpu.make_async_remote_copy(
            src_ref=ref,
            dst_ref=ref,
            send_sem=send_sem,
            recv_sem=recv_sem,
            device_id=device,
            device_id_type=MESH,
        ).wait_recv()

    loads = [
        pltpu.make_async_copy(rk_ref, rkv.at[0, 0], local_sem.at[0]),
        pltpu.make_async_copy(rv_ref, rkv.at[0, 1], local_sem.at[1]),
        pltpu.make_async_copy(pk_ref, pk, local_sem.at[2]),
        pltpu.make_async_copy(pv_ref, pv, local_sem.at[3]),
        pltpu.make_async_copy(sk_ref, sk.at[pl.ds(0, REQ * SUF)], local_sem.at[4]),
        pltpu.make_async_copy(sv_ref, sv.at[pl.ds(0, REQ * SUF)], local_sem.at[5]),
    ]
    for load in loads:
        load.start()

    partners = [at_z(step) for step in range(1, nz)]
    partners += [at_x(step) for step in range(1, NX)]
    if ny > 1:
        partners += [at_y(1), at_y(-1)]
    partners += [sibling]
    barrier = pltpu.get_barrier_semaphore()
    for partner in partners:
        pl.semaphore_signal(barrier, inc=1, device_id=partner, device_id_type=MESH)

    lane1 = iota((1, ROWS), 1)
    stored = [om_ref[0, bl_ref[p % 2, p // 2]] for p in range(2 * REQ)]
    owner = [s // 2 for s in stored]
    code_rows = [jnp.zeros((1, ROWS), jnp.int32), jnp.zeros((1, ROWS), jnp.int32)]
    for p in range(2 * REQ):
        rank = jnp.int32(0)
        for other in range(p):
            rank = rank + (owner[other] == owner[p]).astype(jnp.int32)
        code = owner[p] * 4 + rank * 2 + stored[p] % 2
        code_rows[p % 2] = jnp.where(lane1 // 16 == p // 2, code, code_rows[p % 2])
    metaz[0, pl.ds(0, 1), :] = code_rows[0]
    metaz[0, pl.ds(1, 1), :] = code_rows[1]

    pl.semaphore_wait(barrier, len(partners))

    def q_half(b, h):
        rows = pl.ds(h * HALF, HALF)
        return q_ref.at[rows] if b == 0 else zq.at[b, rows]

    def pass_queries(b, h, step, into):
        send(
            q_half(b, h),
            zq.at[into, pl.ds(h * HALF, HALF)],
            zs_sem.at[into, h],
            zr_sem.at[into, h],
            at_z(step),
        )

    def forward_queries(b, h):
        for step in (1, -1):
            if b == 0 or (step == 1) == (b > zh):
                if b == zh:
                    continue
                into = (b - step) % nz
                if into == zh and h != (0 if step == 1 else 1):
                    continue
                pass_queries(b, h, step, into)

    def query_arrived(b, h):
        arrived(
            zq.at[b, pl.ds(h * HALF, HALF)], zs_sem.at[b, h], zr_sem.at[b, h], at_z(1)
        )

    for h in range(2):
        forward_queries(0, h)
    for step in range(1, nz):
        send(
            metaz.at[0],
            metaz.at[(-step) % nz],
            ms_sem.at[step],
            mr_sem.at[(-step) % nz],
            at_z(step),
        )

    loads[0].wait()
    loads[1].wait()

    def share_root(b):
        send(rkv.at[b], rkv.at[ny + b], cs_sem.at[b], cr_sem.at[b], sibling)

    def forward_root(b):
        for step in (1, -1):
            if b == 0 or (step == 1) == (b > yh):
                if b == yh or ny == 1:
                    continue
                into = (b - step) % ny
                if into == yh:
                    part = 0 if step == 1 else 1
                    send(
                        rkv.at[b, part],
                        rkv.at[into, part],
                        ys_sem.at[into, part],
                        yr_sem.at[into, part],
                        at_y(step),
                    )
                else:
                    send(
                        rkv.at[b],
                        rkv.at[into],
                        ys_sem.at[into, 0],
                        yr_sem.at[into, 0],
                        at_y(step),
                    )

    def root_arrived(b):
        if b == yh:
            for part in range(2):
                arrived(rkv.at[b, part], ys_sem.at[b, part], yr_sem.at[b, part], at_y(1))
        else:
            arrived(rkv.at[b], ys_sem.at[b, 0], yr_sem.at[b, 0], at_y(1))

    forward_root(0)
    share_root(0)

    row = iota((ROWS, ROWS), 0)
    lane = iota((ROWS, ROWS), 1)
    same_place = row % 16 == lane % 16
    diagonal = jnp.where(row == lane, 0.0, DROP)

    def select(b):
        wanted = z * (2 * NX) + row // 16
        first = metaz[b, pl.ds(0, 1), :] // 2
        second = metaz[b, pl.ds(1, 1), :] // 2
        hit = ((first == wanted) | (second == wanted)) & same_place
        onehot[b] = jnp.where(hit, 1.0, 0.0).astype(jnp.bfloat16)
        bias_t[b] = jnp.where(hit, 0.0, DROP).T
        mine = pl.ds(pl.multiple_of(x * SLOT_ROWS, SLOT_ROWS), SLOT_ROWS)

        def body(k, carry):
            block = q_ref[k] if b == 0 else zq[b, k]
            chosen = jnp.dot(onehot[b], block, preferred_element_type=jnp.float32)
            snd[b, k] = chosen.astype(jnp.bfloat16)
            return carry

        lax.fori_loop(0, KV, body, 0, unroll=4)

        def keep(k, carry):
            rcv[b, k, mine, :] = snd[b, k, mine, :]
            return carry

        lax.fori_loop(0, KV, keep, 0, unroll=True)
        for step in range(1, NX):
            there = pl.ds(pl.multiple_of(lax.rem(x + step, NX) * SLOT_ROWS, SLOT_ROWS), SLOT_ROWS)
            send(
                snd.at[b, :, there, :],
                rcv.at[b, :, mine, :],
                xs_sem.at[b, NX - step],
                xr_sem.at[b, NX - step],
                at_x(step),
            )

    def slots_arrived(b):
        for step in range(1, NX):
            there = pl.ds(pl.multiple_of(lax.rem(x + step, NX) * SLOT_ROWS, SLOT_ROWS), SLOT_ROWS)
            arrived(
                rcv.at[b, :, there, :], xs_sem.at[b, step], xr_sem.at[b, step], at_x(step)
            )

    ones_prefix = jnp.ones((BLK, HEAD), jnp.bfloat16)

    def serve(blocks):
        for b in blocks:
            slots_arrived(b)
            for source in range(NX):
                code = metax[source, b]
                srow = iota((SLOT_ROWS, ROWS), 0)
                slane = iota((SLOT_ROWS, ROWS), 1)
                wanted = (dev * 2 + srow // 16) * 2 + 1
                hit = (code[0:1, :] == wanted) | (code[1:2, :] == wanted)
                second = jnp.max(jnp.where(hit, 1.0, 0.0), axis=1, keepdims=True)
                here = pl.ds(source * SLOT_ROWS, SLOT_ROWS)
                pick[b, here, :] = jnp.where(
                    slane == 0, 1.0 - second, jnp.where(slane == 1, second, 0.0)
                ).astype(jnp.bfloat16)
                second_slot[b, here, :] = jnp.broadcast_to(second, (SLOT_ROWS, ROWS))

        def body(k, carry):
            cols = pl.ds(pl.multiple_of(k * HEAD, HEAD), HEAD)
            queries = jnp.concatenate(
                [jnp.concatenate([rcv[b, k], pick[b]], axis=1) for b in blocks], axis=0
            )
            keys = jnp.concatenate([pk[:, cols], kbias[...]], axis=1)
            both = lax.dot_general(queries, keys, NT, preferred_element_type=jnp.float32)
            scores = jnp.maximum(both[:, :BLK], both[:, BLK:])
            highest = jnp.max(scores, axis=1, keepdims=True)
            weights = jnp.exp2((scores - highest) * SCALE2).astype(jnp.bfloat16)
            values = jnp.concatenate([pv[:BLK, cols], pv[BLK:, cols], ones_prefix], axis=1)
            summed = jnp.dot(weights, values, preferred_element_type=jnp.float32)
            totals = summed[:, 2 * HEAD :]
            inverse = 1.0 / totals
            logs = highest * SCALE2 + jnp.log(totals) * LOG2E
            for at, b in enumerate(blocks):
                part = slice(at * ROWS, (at + 1) * ROWS)
                chosen = jnp.where(
                    second_slot[b] > 0.5, summed[part, HEAD : 2 * HEAD], summed[part, :HEAD]
                )
                ans[b, k] = (chosen * inverse[part]).astype(jnp.bfloat16)
                lacc[at] = jnp.where(lane == k, logs[part], lacc[at])
            return carry

        lax.fori_loop(0, KV, body, 0, unroll=2)
        for at, b in enumerate(blocks):
            lmine[b] = lacc[at].T[:KV, :]

    def give_back(b):
        mine = pl.ds(pl.multiple_of(x * SLOT_ROWS, SLOT_ROWS), SLOT_ROWS)
        for step in range(1, NX):
            there = pl.ds(pl.multiple_of(lax.rem(x + step, NX) * SLOT_ROWS, SLOT_ROWS), SLOT_ROWS)
            send(
                ans.at[b, :, there, :],
                ret.at[b, :, mine, :],
                bs_sem.at[b, NX - step],
                br_sem.at[b, NX - step],
                at_x(step),
            )
            send(
                lmine.at[b],
                lret.at[b, NX - step],
                ls_sem.at[b, NX - step],
                lr_sem.at[b, NX - step],
                at_x(step),
            )

        def body(k, carry):
            ret[b, k, mine, :] = ans[b, k, mine, :]
            return carry

        lax.fori_loop(0, KV, body, 0, unroll=True)

    def answers_arrived(b):
        lane8 = iota((KV, ROWS), 1)
        rows = lmine[b]
        for step in range(1, NX):
            there = pl.ds(pl.multiple_of(lax.rem(x + step, NX) * SLOT_ROWS, SLOT_ROWS), SLOT_ROWS)
            arrived(
                ret.at[b, :, there, :], bs_sem.at[b, step], br_sem.at[b, step], at_x(step)
            )
            arrived(lret.at[b, step], ls_sem.at[b, step], lr_sem.at[b, step], at_x(step))
            moved = pltpu.roll(lret[b, step], SLOT_ROWS * step, 1)
            rows = jnp.where(lane8 // SLOT_ROWS == lax.rem(x + step, NX), moved, rows)
        lslot[b] = rows

    def chain(b, h):
        step = 1 if b < zh or (b == zh and h == 0) else -1
        into = (b - step) % nz
        place = into if into else (0 if step == 1 else zh)
        return step, place

    def has_input(b, h):
        return b != zh and (b not in (zh - 1, zh + 1) or chain(zh, h)[1] == b)

    def partial_arrived(place, h):
        arrived(
            rsin.at[place, pl.ds(h * HALF, HALF)],
            rs_sem.at[place, h],
            rr_sem.at[place, h],
            at_z(1),
        )
        arrived(lin.at[place, h], es_sem.at[place, h], er_sem.at[place, h], at_z(1))

    def combine(blocks, h):
        for b in blocks:
            if has_input(b, h):
                partial_arrived(b, h)

        def body(k, carry):
            for at, b in enumerate(blocks):
                rows = jnp.broadcast_to(lslot[b, pl.ds(k, 1), :], (ROWS, ROWS)) + bias_t[b]
                parts = ret[b, k]
                if has_input(b, h):
                    extra = jnp.broadcast_to(lin[b, h, pl.ds(k, 1), :], (ROWS, ROWS)) + diagonal
                    rows = jnp.concatenate([rows, extra], axis=1)
                    parts = jnp.concatenate([parts, rsin[b, k]], axis=0)
                highest = jnp.maximum(jnp.max(rows, axis=1, keepdims=True), FLOOR)
                weights = jnp.exp2(rows - highest).astype(jnp.bfloat16)
                parts = jnp.concatenate([parts, jnp.ones_like(parts)], axis=1)
                summed = jnp.dot(weights, parts, preferred_element_type=jnp.float32)
                totals = jnp.maximum(summed[:, HEAD:], 1.0e-30)
                rsout[b, k] = (summed[:, :HEAD] / totals).astype(jnp.bfloat16)
                lacc[at] = jnp.where(lane == k, highest + jnp.log(totals) * LOG2E, lacc[at])
            return carry

        lax.fori_loop(h * HALF, (h + 1) * HALF, body, 0, unroll=2)
        for at, b in enumerate(blocks):
            lout[b, h] = lacc[at].T[:KV, :]
            step, place = chain(b, h)
            part = pl.ds(h * HALF, HALF)
            send(
                rsout.at[b, part],
                rsin.at[place, part],
                rs_sem.at[place, h],
                rr_sem.at[place, h],
                at_z(step),
            )
            send(
                lout.at[b, h],
                lin.at[place, h],
                es_sem.at[place, h],
                er_sem.at[place, h],
                at_z(step),
            )

    ones_root = jnp.ones((ny * CORES * rkv.shape[2], HEAD), jnp.bfloat16)
    ones_local = jnp.ones((LOCAL, HEAD), jnp.bfloat16)
    root_rows = ny * CORES * rkv.shape[2]

    def attend_local(k_from, k_to):
        def body(k, carry):
            cols = pl.ds(pl.multiple_of(k * HEAD, HEAD), HEAD)
            queries = q_ref[k]
            root_keys = rkv[:, 0, :, cols].reshape(root_rows, HEAD)
            root_values = rkv[:, 1, :, cols].reshape(root_rows, HEAD)
            root_scores = lax.dot_general(
                queries, root_keys, NT, preferred_element_type=jnp.float32
            )
            wide = jnp.concatenate([queries, lpick[...]], axis=1)
            keys = jnp.concatenate([sk[:, cols], lbias[...]], axis=1)
            scores = lax.dot_general(wide, keys, NT, preferred_element_type=jnp.float32)
            highest = jnp.maximum(
                jnp.max(root_scores, axis=1, keepdims=True),
                jnp.max(scores, axis=1, keepdims=True),
            )
            root_weights = jnp.exp2((root_scores - highest) * SCALE2).astype(jnp.bfloat16)
            weights = jnp.exp2((scores - highest) * SCALE2).astype(jnp.bfloat16)
            summed = jnp.dot(
                root_weights,
                jnp.concatenate([root_values, ones_root], axis=1),
                preferred_element_type=jnp.float32,
            ) + jnp.dot(
                weights,
                jnp.concatenate([sv[:, cols], ones_local], axis=1),
                preferred_element_type=jnp.float32,
            )
            loc_acc[k] = summed[:, :HEAD]
            loc_tot[k] = summed[:, HEAD:]
            loc_max[k] = jnp.broadcast_to(highest * SCALE2, (ROWS, ROWS))
            return carry

        lax.fori_loop(k_from, k_to, body, 0)

    def finish(h):
        partial_arrived(0, h)
        partial_arrived(zh, h)

        def body(k, carry):
            rows = jnp.concatenate(
                [
                    jnp.broadcast_to(lslot[0, pl.ds(k, 1), :], (ROWS, ROWS)) + bias_t[0],
                    jnp.broadcast_to(lin[0, h, pl.ds(k, 1), :], (ROWS, ROWS)) + diagonal,
                    jnp.broadcast_to(lin[zh, h, pl.ds(k, 1), :], (ROWS, ROWS)) + diagonal,
                ],
                axis=1,
            )
            highest = jnp.maximum(jnp.max(rows, axis=1, keepdims=True), loc_max[k])
            wide = jnp.concatenate([highest] * 3, axis=1)
            weights = jnp.exp2(rows - wide).astype(jnp.bfloat16)
            parts = jnp.concatenate([ret[0, k], rsin[0, k], rsin[zh, k]], axis=0)
            parts = jnp.concatenate([parts, jnp.ones_like(parts)], axis=1)
            summed = jnp.dot(weights, parts, preferred_element_type=jnp.float32)
            share = jnp.exp2(loc_max[k] - highest)
            numerator = summed[:, :HEAD] + loc_acc[k] * share
            denominator = summed[:, HEAD:] + loc_tot[k] * share
            out_ref[k] = (numerator / denominator).astype(jnp.bfloat16)
            return carry

        lax.fori_loop(h * HALF, (h + 1) * HALF, body, 0, unroll=2)

    lacc[...] = jnp.zeros_like(lacc)
    select(0)

    for b in range(1, nz):
        arrived(metaz.at[b], ms_sem.at[b], mr_sem.at[b], at_z(1))
    for step in range(1, NX):
        send(
            metaz,
            metax.at[x],
            nsend_sem.at[NX - step],
            nrecv_sem.at[NX - step],
            at_x(step),
        )
    metax[x] = metaz[...]

    prow = iota((2 * BLK, HEAD), 0)
    plane = iota((2 * BLK, HEAD), 1)
    limit = jnp.where(prow < BLK, plen_ref[0], plen_ref[1])
    live = prow % BLK < limit
    kbias[...] = jnp.where(
        (plane < 2) & ~((plane == prow // BLK) & live), DROP, 0.0
    ).astype(jnp.bfloat16)
    lrow = iota((LOCAL, HEAD), 0)
    llane = iota((LOCAL, HEAD), 1)
    length = jnp.zeros((LOCAL, HEAD), jnp.int32)
    for r in range(REQ):
        length = jnp.where(lrow // SUF == r, slen_ref[r], length)
    past = (lrow < REQ * SUF) & (llane // 2 == lrow // SUF) & (lrow % SUF < length)
    fresh_row = lrow - REQ * SUF
    fresh = (
        (fresh_row >= 0) & (llane // 2 == fresh_row // 16) & (fresh_row % 16 <= llane % 2)
    )
    lbias[...] = jnp.where((llane < 2 * REQ) & ~(past | fresh), DROP, 0.0).astype(jnp.bfloat16)
    lpick[...] = jnp.where(lane == row // 8, 1.0, 0.0).astype(jnp.bfloat16)
    for cache, new in ((sk, nk_ref), (sv, nv_ref)):
        cache[pl.ds(REQ * SUF, 16 * REQ), :] = jnp.zeros((16 * REQ, KV * HEAD), jnp.bfloat16)
        for r in range(REQ):
            cache[pl.ds(REQ * SUF + 16 * r, 2), :] = new[r]

    for load in loads[2:]:
        load.wait()
    meta_waited = False

    waiting = (0,)
    for s in range(1, zh + 1):
        blocks = (nz - s, s) if s < zh else (zh,)
        for h in range(2):
            for b in blocks:
                query_arrived(b, h)
                forward_queries(b, h)
        for b in blocks:
            select(b)
        if s <= yh:
            for b in (ny - s, s) if s < yh else (yh,):
                root_arrived(b)
                forward_root(b)
                share_root(b)
        if not meta_waited:
            meta_waited = True
            for step in range(1, NX):
                arrived(
                    metax.at[lax.rem(x + step, NX)],
                    nsend_sem.at[step],
                    nrecv_sem.at[step],
                    at_x(step),
                )
        serve(waiting)
        waiting = blocks
    for s in range(zh + 1, yh + 1):
        for b in (ny - s, s) if s < yh else (yh,):
            root_arrived(b)
            forward_root(b)
            share_root(b)

    serve(waiting)
    give_back(zh)
    order = [(zh,)] + [(s, nz - s) for s in range(zh - 1, 0, -1)] + [(0,)]
    for b in order[1]:
        give_back(b)

    for b in range(ny):
        arrived(rkv.at[ny + b], cs_sem.at[b], cr_sem.at[b], sibling)
    shares = [KV * (turn + 1) // zh for turn in range(zh)]
    for turn, blocks in enumerate(order[:-1]):
        if turn == 0:
            attend_local(0, shares[0])
        for b in blocks:
            answers_arrived(b)
        for h in range(2):
            combine(blocks, h)
        if turn + 2 < len(order):
            for b in order[turn + 2]:
                give_back(b)
        if turn:
            attend_local(shares[turn - 1], shares[turn])
    answers_arrived(0)
    for h in range(2):
        finish(h)

    for copy in drains:
        copy.wait_send()


def shards(nz, ny, *args):
    (
        queries,
        new_keys,
        new_values,
        suffix_keys,
        suffix_values,
        suffix_lengths,
        root_keys,
        root_values,
        prefix_keys,
        prefix_values,
        prefix_lengths,
        owner_map,
        block_lists,
    ) = args
    width = KV * HEAD
    head_major = (
        queries.reshape(REQ, 2, KV, 8, HEAD).transpose(2, 0, 1, 3, 4).reshape(KV, ROWS, HEAD)
    )
    root_rows = root_keys.shape[0]
    bf16, f32 = jnp.bfloat16, jnp.float32
    vmem = pl.BlockSpec(memory_space=pltpu.VMEM)
    smem = pl.BlockSpec(memory_space=pltpu.SMEM)
    anywhere = pl.BlockSpec(memory_space=pl.ANY)
    dma = pltpu.SemaphoreType.DMA
    blocks = (nz, KV, ROWS, HEAD)
    out = pl.pallas_call(
        functools.partial(kernel, nz, ny),
        out_shape=jax.ShapeDtypeStruct((KV, ROWS, HEAD), bf16),
        in_specs=[vmem, vmem, vmem] + [anywhere] * 6 + [smem] * 4,
        out_specs=vmem,
        scratch_shapes=[
            pltpu.VMEM(blocks, bf16),
            pltpu.VMEM(blocks, bf16),
            pltpu.VMEM(blocks, bf16),
            pltpu.VMEM(blocks, bf16),
            pltpu.VMEM(blocks, bf16),
            pltpu.VMEM(blocks, bf16),
            pltpu.VMEM(blocks, bf16),
            pltpu.VMEM((2 * ny, 2, root_rows, width), bf16),
            pltpu.VMEM((2 * BLK, width), bf16),
            pltpu.VMEM((2 * BLK, width), bf16),
            pltpu.VMEM((LOCAL, width), bf16),
            pltpu.VMEM((LOCAL, width), bf16),
            pltpu.VMEM((nz, 2, ROWS), jnp.int32),
            pltpu.VMEM((NX, nz, 2, ROWS), jnp.int32),
            pltpu.VMEM((nz, ROWS, ROWS), bf16),
            pltpu.VMEM((nz, ROWS, ROWS), f32),
            pltpu.VMEM((nz, ROWS, HEAD), bf16),
            pltpu.VMEM((2 * BLK, HEAD), bf16),
            pltpu.VMEM((LOCAL, HEAD), bf16),
            pltpu.VMEM((ROWS, HEAD), bf16),
            pltpu.VMEM((nz, KV, ROWS), f32),
            pltpu.VMEM((nz, NX, KV, ROWS), f32),
            pltpu.VMEM((nz, KV, ROWS), f32),
            pltpu.VMEM((nz, 2, KV, ROWS), f32),
            pltpu.VMEM((nz, 2, KV, ROWS), f32),
            pltpu.VMEM((KV, ROWS, HEAD), f32),
            pltpu.VMEM((KV, ROWS, HEAD), f32),
            pltpu.VMEM((KV, ROWS, HEAD), f32),
            pltpu.VMEM((2, ROWS, ROWS), f32),
            pltpu.VMEM((nz, ROWS, ROWS), f32),
            dma((6,)),
            dma((nz, 2)),
            dma((nz, 2)),
            dma((nz,)),
            dma((nz,)),
            dma((NX,)),
            dma((NX,)),
            dma((nz, NX)),
            dma((nz, NX)),
            dma((nz, NX)),
            dma((nz, NX)),
            dma((nz, NX)),
            dma((nz, NX)),
            dma((nz, 2)),
            dma((nz, 2)),
            dma((nz, 2)),
            dma((nz, 2)),
            dma((ny, 2)),
            dma((ny, 2)),
            dma((ny,)),
            dma((ny,)),
        ],
        compiler_params=pltpu.CompilerParams(
            collective_id=0, has_side_effects=True, vmem_limit_bytes=60 * 1024 * 1024 + 512 * 1024
        ),
        cost_estimate=pl.CostEstimate(
            flops=4_000_000_000, bytes_accessed=5_000_000, transcendentals=8_000_000
        ),
        name="shared_prefix_attention",
    )(
        head_major,
        new_keys,
        new_values,
        suffix_keys.reshape(REQ * SUF, width),
        suffix_values.reshape(REQ * SUF, width),
        root_keys,
        root_values,
        prefix_keys.reshape(2 * BLK, width),
        prefix_values.reshape(2 * BLK, width),
        suffix_lengths,
        prefix_lengths,
        owner_map,
        block_lists.T,
    )
    return out.reshape(KV, REQ, 2, 8, HEAD).transpose(1, 2, 0, 3, 4).reshape(REQ, 2, 64 * HEAD)


def solution(mesh):
    return jax.shard_map(
        functools.partial(shards, mesh.shape["dev"] // NX, mesh.shape["group"] // CORES),
        mesh=mesh,
        in_specs=(
            P(("group", "dev"), None, None),
            P(("group", "dev"), None, None),
            P(("group", "dev"), None, None),
            P(("group", "dev"), None, None),
            P(("group", "dev"), None, None),
            P(("group", "dev")),
            P("group", None),
            P("group", None),
            P(("group", "dev"), None, None),
            P(("group", "dev"), None, None),
            P(("group", "dev")),
            P("group", None),
            P(("group", "dev"), None),
        ),
        out_specs=P(("group", "dev"), None, None),
        check_vma=False,
    )
```

```python
import functools
import math

import jax
import jax.numpy as jnp
from jax import lax
from jax.experimental import pallas as pl
from jax.experimental.pallas import tpu as pltpu
from jax.sharding import PartitionSpec as P

KV = 8
HEAD = 128
NX = 4
CORES = 2
REQ = 8
ROWS = 128
SLOT_ROWS = 32
BLK = 256
SUF = 32
LOCAL = 384
HALF = KV // 2
FLOOR = -1.0e30
DROP = -2.0e30
SCALE = 1.0 / math.sqrt(HEAD)
LOG2E = 1.0 / math.log(2.0)
SCALE2 = SCALE * LOG2E
MESH = pl.DeviceIdType.MESH
NT = (((1,), (1,)), ((), ()))


def iota(shape, dim):
    return lax.broadcasted_iota(jnp.int32, shape, dim)


def kernel(
    nz,
    ny,
    q_ref,
    nk_ref,
    nv_ref,
    sk_ref,
    sv_ref,
    rk_ref,
    rv_ref,
    pk_ref,
    pv_ref,
    slen_ref,
    plen_ref,
    om_ref,
    bl_ref,
    out_ref,
    zq,
    snd,
    rcv,
    ans,
    ret,
    rsin,
    rsout,
    rkv,
    pk,
    pv,
    sk,
    sv,
    metaz,
    metax,
    onehot,
    bias_t,
    pick,
    kbias,
    lbias,
    lpick,
    lmine,
    lret,
    lslot,
    lin,
    lout,
    loc_acc,
    loc_max,
    loc_tot,
    lacc,
    second_slot,
    score_even,
    score_odd,
    local_sem,
    sent_sem,
    all_sem,
    zr_sem,
    xr_sem,
    br_sem,
    lr_sem,
    rr_sem,
    er_sem,
    yr_sem,
):
    zh = nz // 2
    yh = ny // 2
    group = lax.axis_index("group")
    dev = lax.axis_index("dev")
    z, x = dev // NX, dev % NX
    y, core = group // CORES, group % CORES

    def at_z(step):
        return (group, lax.rem(z + step + nz, nz) * NX + x)

    def at_x(step):
        return (group, z * NX + lax.rem(x + step, NX))

    def at_y(step):
        return (lax.rem(y + step + ny, ny) * CORES + core, dev)

    sibling = (y * CORES + 1 - core, dev)

    def send(src, dst, send_sem, recv_sem, device):
        pltpu.make_async_remote_copy(
            src_ref=src,
            dst_ref=dst,
            send_sem=send_sem,
            recv_sem=recv_sem,
            device_id=device,
            device_id_type=MESH,
        ).start()

    def arrived(ref, recv_sem):
        pltpu.make_async_copy(ref, ref, recv_sem).wait()

    loads = [
        pltpu.make_async_copy(rk_ref, rkv.at[0, 0], local_sem.at[0]),
        pltpu.make_async_copy(rv_ref, rkv.at[0, 1], local_sem.at[1]),
        pltpu.make_async_copy(pk_ref, pk, local_sem.at[2]),
        pltpu.make_async_copy(pv_ref, pv, local_sem.at[3]),
        pltpu.make_async_copy(sk_ref, sk.at[pl.ds(0, REQ * SUF)], local_sem.at[4]),
        pltpu.make_async_copy(sv_ref, sv.at[pl.ds(0, REQ * SUF)], local_sem.at[5]),
    ]
    for load in loads:
        load.start()

    partners = [at_z(step) for step in range(1, nz)]
    partners += [at_x(step) for step in range(1, NX)]
    if ny > 1:
        partners += [at_y(1), at_y(-1)]
    partners += [sibling]
    barrier = pltpu.get_barrier_semaphore()
    for partner in partners:
        pl.semaphore_signal(barrier, inc=1, device_id=partner, device_id_type=MESH)

    lane1 = iota((1, ROWS), 1)
    stored = [om_ref[0, bl_ref[p % 2, p // 2]] for p in range(2 * REQ)]
    owner = [s // 2 for s in stored]
    code_rows = [jnp.zeros((1, ROWS), jnp.int32), jnp.zeros((1, ROWS), jnp.int32)]
    for p in range(2 * REQ):
        rank = jnp.int32(0)
        for other in range(p):
            rank = rank + (owner[other] == owner[p]).astype(jnp.int32)
        code = owner[p] * 4 + rank * 2 + stored[p] % 2
        code_rows[p % 2] = jnp.where(lane1 // 16 == p // 2, code, code_rows[p % 2])
    metaz[0, pl.ds(0, 1), :] = code_rows[0]
    metaz[0, pl.ds(1, 1), :] = code_rows[1]

    pl.semaphore_wait(barrier, len(partners))

    def q_half(b, h):
        rows = pl.ds(h * HALF, HALF)
        return q_ref.at[rows] if b == 0 else zq.at[b, rows]

    def pass_queries(b, h, step, into):
        send(
            q_half(b, h),
            zq.at[into, pl.ds(h * HALF, HALF)],
            sent_sem.at[0],
            zr_sem.at[into, h],
            at_z(step),
        )

    def forward_queries(b, h):
        for step in (1, -1):
            if b == 0 or (step == 1) == (b > zh):
                if b == zh:
                    continue
                into = (b - step) % nz
                if into == zh and h != (0 if step == 1 else 1):
                    continue
                pass_queries(b, h, step, into)

    def query_arrived(b, h):
        arrived(zq.at[b, pl.ds(h * HALF, HALF)], zr_sem.at[b, h])

    for h in range(2):
        forward_queries(0, h)
    for step in range(1, nz):
        send(
            metaz.at[0],
            metaz.at[(-step) % nz],
            sent_sem.at[1],
            all_sem.at[0],
            at_z(step),
        )

    loads[0].wait()
    loads[1].wait()

    def share_root(b):
        send(rkv.at[b], rkv.at[ny + b], sent_sem.at[2], all_sem.at[1], sibling)

    def forward_root(b):
        for step in (1, -1):
            if b == 0 or (step == 1) == (b > yh):
                if b == yh or ny == 1:
                    continue
                into = (b - step) % ny
                if into == yh:
                    part = 0 if step == 1 else 1
                    send(
                        rkv.at[b, part],
                        rkv.at[into, part],
                        sent_sem.at[3],
                        yr_sem.at[into, part],
                        at_y(step),
                    )
                else:
                    send(
                        rkv.at[b],
                        rkv.at[into],
                        sent_sem.at[3],
                        yr_sem.at[into, 0],
                        at_y(step),
                    )

    def root_arrived(b):
        if b == yh:
            for part in range(2):
                arrived(rkv.at[b, part], yr_sem.at[b, part])
        else:
            arrived(rkv.at[b], yr_sem.at[b, 0])

    forward_root(0)
    share_root(0)

    row = iota((ROWS, ROWS), 0)
    lane = iota((ROWS, ROWS), 1)
    same_place = row % 16 == lane % 16
    diagonal = jnp.where(row == lane, 0.0, DROP)

    def there(step):
        return pl.ds(pl.multiple_of(lax.rem(x + step, NX) * SLOT_ROWS, SLOT_ROWS), SLOT_ROWS)

    mine = there(0)
    others = pl.ds(0, (NX - 1) * SLOT_ROWS)

    def route(b):
        wanted = z * (2 * NX) + row // 16
        first = metaz[b, pl.ds(0, 1), :] // 2
        second = metaz[b, pl.ds(1, 1), :] // 2
        hit = ((first == wanted) | (second == wanted)) & same_place
        onehot[b] = jnp.where(hit, 1.0, 0.0).astype(jnp.bfloat16)
        bias_t[b] = jnp.where(hit, 0.0, DROP).T

    def select(b, h):
        part = pl.ds(h * HALF, HALF)

        def body(k, carry):
            block = q_ref[k] if b == 0 else zq[b, k]
            chosen = jnp.dot(onehot[b], block, preferred_element_type=jnp.float32)
            snd[b, k] = chosen.astype(jnp.bfloat16)
            return carry

        lax.fori_loop(h * HALF, (h + 1) * HALF, body, 0, unroll=True)
        for step in range(1, NX):
            send(
                snd.at[b, part, there(step), :],
                rcv.at[b, part, mine, :],
                sent_sem.at[4],
                xr_sem.at[b, h],
                at_x(step),
            )

        def keep(k, carry):
            rcv[b, k, mine, :] = snd[b, k, mine, :]
            return carry

        lax.fori_loop(h * HALF, (h + 1) * HALF, keep, 0, unroll=True)

    def slots_arrived(b, h):
        arrived(rcv.at[b, pl.ds(h * HALF, HALF), others, :], xr_sem.at[b, h])

    ones_prefix = jnp.ones((BLK, HEAD), jnp.bfloat16)

    def label_slots(b):
        for source in range(NX):
            code = metax[source, b]
            srow = iota((SLOT_ROWS, ROWS), 0)
            slane = iota((SLOT_ROWS, ROWS), 1)
            wanted = (dev * 2 + srow // 16) * 2 + 1
            hit = (code[0:1, :] == wanted) | (code[1:2, :] == wanted)
            second = jnp.max(jnp.where(hit, 1.0, 0.0), axis=1, keepdims=True)
            here = pl.ds(source * SLOT_ROWS, SLOT_ROWS)
            pick[b, here, :] = jnp.where(
                slane == 0, 1.0 - second, jnp.where(slane == 1, second, 0.0)
            ).astype(jnp.bfloat16)
            second_slot[b, here, :] = jnp.broadcast_to(second, (SLOT_ROWS, ROWS))

    def serve(blocks, halves):
        rows = len(blocks) * ROWS
        last = HALF * (halves[-1] + 1) - 1

        def score(k, into):
            cols = pl.ds(pl.multiple_of(k * HEAD, HEAD), HEAD)
            queries = jnp.concatenate(
                [jnp.concatenate([rcv[b, k], pick[b]], axis=1) for b in blocks], axis=0
            )
            keys = jnp.concatenate([pk[:, cols], kbias[...]], axis=1)
            both = lax.dot_general(queries, keys, NT, preferred_element_type=jnp.float32)
            into[pl.ds(0, rows), :] = jnp.maximum(both[:, :BLK], both[:, BLK:])

        def weigh(k, source):
            cols = pl.ds(pl.multiple_of(k * HEAD, HEAD), HEAD)
            scores = source[pl.ds(0, rows), :]
            highest = jnp.max(scores, axis=1, keepdims=True)
            weights = jnp.exp2((scores - highest) * SCALE2).astype(jnp.bfloat16)
            values = jnp.concatenate([pv[:BLK, cols], pv[BLK:, cols], ones_prefix], axis=1)
            summed = jnp.dot(weights, values, preferred_element_type=jnp.float32)
            totals = summed[:, 2 * HEAD :]
            inverse = 1.0 / totals
            logs = highest * SCALE2 + jnp.log(totals) * LOG2E
            for at, b in enumerate(blocks):
                part = slice(at * ROWS, (at + 1) * ROWS)
                chosen = jnp.where(
                    second_slot[b] > 0.5, summed[part, HEAD : 2 * HEAD], summed[part, :HEAD]
                )
                ans[b, k] = (chosen * inverse[part]).astype(jnp.bfloat16)
                lacc[at] = jnp.where(lane == k, logs[part], lacc[at])

        def body(turn, carry):
            k = HALF * halves[0] + 2 * turn
            score(k + 1, score_odd)
            weigh(k, score_even)
            score(jnp.minimum(k + 2, last), score_even)
            weigh(k + 1, score_odd)
            return carry

        score(HALF * halves[0], score_even)
        lax.fori_loop(0, len(halves) * HALF // 2, body, 0)
        for at, b in enumerate(blocks):
            logs = lacc[at].T[:KV, :]
            for h in halves:
                lmine[b, h] = logs

    def give_back(b, h):
        part = pl.ds(h * HALF, HALF)
        for step in range(1, NX):
            send(
                ans.at[b, part, there(step), :],
                ret.at[b, part, mine, :],
                sent_sem.at[5],
                br_sem.at[b, h],
                at_x(step),
            )
            send(
                lmine.at[b, h],
                lret.at[b, h, NX - step],
                sent_sem.at[6],
                lr_sem.at[b, h],
                at_x(step),
            )

        def body(k, carry):
            ret[b, k, mine, :] = ans[b, k, mine, :]
            return carry

        lax.fori_loop(h * HALF, (h + 1) * HALF, body, 0, unroll=True)

    def answers_arrived(b, h):
        lane8 = iota((KV, ROWS), 1)
        rows = lmine[b, h]
        arrived(ret.at[b, pl.ds(h * HALF, HALF), others, :], br_sem.at[b, h])
        arrived(lret.at[b, h, pl.ds(1, NX - 1)], lr_sem.at[b, h])
        for step in range(1, NX):
            moved = pltpu.roll(lret[b, h, step], SLOT_ROWS * step, 1)
            rows = jnp.where(lane8 // SLOT_ROWS == lax.rem(x + step, NX), moved, rows)
        lslot[b, h] = rows

    def chain(b, h):
        step = 1 if b < zh or (b == zh and h == 0) else -1
        into = (b - step) % nz
        place = into if into else (0 if step == 1 else zh)
        return step, place

    def has_input(b, h):
        return b != zh and (b not in (zh - 1, zh + 1) or chain(zh, h)[1] == b)

    def partial_arrived(place, h):
        arrived(rsin.at[place, pl.ds(h * HALF, HALF)], rr_sem.at[place, h])
        arrived(lin.at[place, h], er_sem.at[place, h])

    def combine(blocks, h):
        for b in blocks:
            if has_input(b, h):
                partial_arrived(b, h)

        def body(k, carry):
            def logs(b):
                rows = jnp.broadcast_to(lslot[b, h, pl.ds(k, 1), :], (ROWS, ROWS)) + bias_t[b]
                if has_input(b, h):
                    extra = jnp.broadcast_to(lin[b, h, pl.ds(k, 1), :], (ROWS, ROWS)) + diagonal
                    rows = jnp.concatenate([rows, extra], axis=1)
                return rows

            highest = [
                jnp.maximum(jnp.max(logs(b), axis=1, keepdims=True), FLOOR) for b in blocks
            ]
            weights = [jnp.exp2(logs(b) - top).astype(jnp.bfloat16) for b, top in zip(blocks, highest)]
            sums = []
            for b, weight in zip(blocks, weights):
                parts = ret[b, k]
                if has_input(b, h):
                    parts = jnp.concatenate([parts, rsin[b, k]], axis=0)
                parts = jnp.concatenate([parts, jnp.ones_like(parts)], axis=1)
                sums.append(jnp.dot(weight, parts, preferred_element_type=jnp.float32))
            for at, b in enumerate(blocks):
                totals = jnp.maximum(sums[at][:, HEAD:], 1.0e-30)
                rsout[b, k] = (sums[at][:, :HEAD] / totals).astype(jnp.bfloat16)
                lacc[at] = jnp.where(lane == k, highest[at] + jnp.log(totals) * LOG2E, lacc[at])
            return carry

        lax.fori_loop(h * HALF, (h + 1) * HALF, body, 0, unroll=2)
        for at, b in enumerate(blocks):
            lout[b, h] = lacc[at].T[:KV, :]
            step, place = chain(b, h)
            part = pl.ds(h * HALF, HALF)
            send(
                rsout.at[b, part],
                rsin.at[place, part],
                sent_sem.at[7],
                rr_sem.at[place, h],
                at_z(step),
            )
            send(
                lout.at[b, h],
                lin.at[place, h],
                sent_sem.at[8],
                er_sem.at[place, h],
                at_z(step),
            )

    ones_root = jnp.ones((ny * CORES * rkv.shape[2], HEAD), jnp.bfloat16)
    ones_local = jnp.ones((LOCAL, HEAD), jnp.bfloat16)
    root_rows = ny * CORES * rkv.shape[2]

    def attend_local(k_from, k_to):
        def body(k, carry):
            cols = pl.ds(pl.multiple_of(k * HEAD, HEAD), HEAD)
            queries = q_ref[k]
            root_keys = rkv[:, 0, :, cols].reshape(root_rows, HEAD)
            root_values = rkv[:, 1, :, cols].reshape(root_rows, HEAD)
            root_scores = lax.dot_general(
                queries, root_keys, NT, preferred_element_type=jnp.float32
            )
            wide = jnp.concatenate([queries, lpick[...]], axis=1)
            keys = jnp.concatenate([sk[:, cols], lbias[...]], axis=1)
            scores = lax.dot_general(wide, keys, NT, preferred_element_type=jnp.float32)
            highest = jnp.maximum(
                jnp.max(root_scores, axis=1, keepdims=True),
                jnp.max(scores, axis=1, keepdims=True),
            )
            root_weights = jnp.exp2((root_scores - highest) * SCALE2).astype(jnp.bfloat16)
            weights = jnp.exp2((scores - highest) * SCALE2).astype(jnp.bfloat16)
            summed = jnp.dot(
                root_weights,
                jnp.concatenate([root_values, ones_root], axis=1),
                preferred_element_type=jnp.float32,
            ) + jnp.dot(
                weights,
                jnp.concatenate([sv[:, cols], ones_local], axis=1),
                preferred_element_type=jnp.float32,
            )
            loc_acc[k] = summed[:, :HEAD]
            loc_tot[k] = summed[:, HEAD:]
            loc_max[k] = jnp.broadcast_to(highest * SCALE2, (ROWS, ROWS))
            return carry

        lax.fori_loop(k_from, k_to, body, 0)

    def finish(h):
        partial_arrived(0, h)
        partial_arrived(zh, h)

        def body(k, carry):
            rows = jnp.concatenate(
                [
                    jnp.broadcast_to(lslot[0, h, pl.ds(k, 1), :], (ROWS, ROWS)) + bias_t[0],
                    jnp.broadcast_to(lin[0, h, pl.ds(k, 1), :], (ROWS, ROWS)) + diagonal,
                    jnp.broadcast_to(lin[zh, h, pl.ds(k, 1), :], (ROWS, ROWS)) + diagonal,
                ],
                axis=1,
            )
            highest = jnp.maximum(jnp.max(rows, axis=1, keepdims=True), loc_max[k])
            wide = jnp.concatenate([highest] * 3, axis=1)
            weights = jnp.exp2(rows - wide).astype(jnp.bfloat16)
            parts = jnp.concatenate([ret[0, k], rsin[0, k], rsin[zh, k]], axis=0)
            parts = jnp.concatenate([parts, jnp.ones_like(parts)], axis=1)
            summed = jnp.dot(weights, parts, preferred_element_type=jnp.float32)
            share = jnp.exp2(loc_max[k] - highest)
            numerator = summed[:, :HEAD] + loc_acc[k] * share
            denominator = summed[:, HEAD:] + loc_tot[k] * share
            out_ref[k] = (numerator / denominator).astype(jnp.bfloat16)
            return carry

        lax.fori_loop(h * HALF, (h + 1) * HALF, body, 0, unroll=2)

    lacc[...] = jnp.zeros_like(lacc)
    route(0)
    for h in range(2):
        select(0, h)

    arrived(metaz.at[pl.ds(1, nz - 1)], all_sem.at[0])
    for step in range(1, NX):
        send(
            metaz,
            metax.at[x],
            sent_sem.at[9],
            all_sem.at[2],
            at_x(step),
        )
    metax[x] = metaz[...]

    prow = iota((2 * BLK, HEAD), 0)
    plane = iota((2 * BLK, HEAD), 1)
    limit = jnp.where(prow < BLK, plen_ref[0], plen_ref[1])
    live = prow % BLK < limit
    kbias[...] = jnp.where(
        (plane < 2) & ~((plane == prow // BLK) & live), DROP, 0.0
    ).astype(jnp.bfloat16)
    lrow = iota((LOCAL, HEAD), 0)
    llane = iota((LOCAL, HEAD), 1)
    length = jnp.zeros((LOCAL, HEAD), jnp.int32)
    for r in range(REQ):
        length = jnp.where(lrow // SUF == r, slen_ref[r], length)
    past = (lrow < REQ * SUF) & (llane // 2 == lrow // SUF) & (lrow % SUF < length)
    fresh_row = lrow - REQ * SUF
    fresh = (
        (fresh_row >= 0) & (llane // 2 == fresh_row // 16) & (fresh_row % 16 <= llane % 2)
    )
    lbias[...] = jnp.where((llane < 2 * REQ) & ~(past | fresh), DROP, 0.0).astype(jnp.bfloat16)
    lpick[...] = jnp.where(lane == row // 8, 1.0, 0.0).astype(jnp.bfloat16)
    for cache, new in ((sk, nk_ref), (sv, nv_ref)):
        cache[pl.ds(REQ * SUF, 16 * REQ), :] = jnp.zeros((16 * REQ, KV * HEAD), jnp.bfloat16)
        for r in range(REQ):
            cache[pl.ds(REQ * SUF + 16 * r, 2), :] = new[r]

    for load in loads[2:]:
        load.wait()
    for b in range(1, nz):
        route(b)

    def advance_root(s):
        for b in (ny - s, s) if s < yh else (yh,):
            root_arrived(b)
            forward_root(b)
            share_root(b)

    waiting = (0,)
    for s in range(1, zh + 1):
        blocks = (nz - s, s) if s < zh else (zh,)
        for h in range(2):
            for b in blocks:
                query_arrived(b, h)
                forward_queries(b, h)
            for b in blocks:
                select(b, h)
        if s <= yh:
            advance_root(s)
        if s == 1:
            arrived(metax.at[pl.ds(0, NX - 1)], all_sem.at[2])
            for b in range(nz):
                label_slots(b)
        for b in waiting:
            for h in range(2):
                slots_arrived(b, h)
        serve(waiting, (0, 1))
        waiting = blocks
    for s in range(zh + 1, yh + 1):
        advance_root(s)

    order = [(zh,)] + [(s, nz - s) for s in range(zh - 1, 0, -1)] + [(0,)]
    for h in range(2):
        slots_arrived(zh, h)
        serve((zh,), (h,))
        give_back(zh, h)

    arrived(rkv.at[pl.ds(ny, ny)], all_sem.at[1])
    shares = [KV * (turn + 1) // zh for turn in range(zh)]
    attend_local(0, shares[0])
    for turn, blocks in enumerate(order[:-1]):
        for h in range(2):
            if turn == 0:
                for b in order[1]:
                    give_back(b, h)
            for b in blocks:
                answers_arrived(b, h)
            combine(blocks, h)
            if turn + 2 < len(order):
                for b in order[turn + 2]:
                    give_back(b, h)
        if turn:
            attend_local(shares[turn - 1], shares[turn])
    for h in range(2):
        answers_arrived(0, h)
        finish(h)

    for at, ref in enumerate(
        (
            zq.at[pl.ds(1, nz - 1)],
            metaz.at[pl.ds(1, nz - 1)],
            rkv.at[pl.ds(0, ny)],
            rkv.at[pl.ds(1, ny - 1)],
            rcv.at[:, :, others, :],
            ret.at[:, :, others, :],
            lret.at[:, :, pl.ds(1, NX - 1)],
            rsin.at[pl.ds(1, nz - 1)],
            lin.at[pl.ds(1, nz - 1)],
            metax.at[pl.ds(1, NX - 1)],
        )
    ):
        arrived(ref, sent_sem.at[at])


def shards(nz, ny, *args):
    (
        queries,
        new_keys,
        new_values,
        suffix_keys,
        suffix_values,
        suffix_lengths,
        root_keys,
        root_values,
        prefix_keys,
        prefix_values,
        prefix_lengths,
        owner_map,
        block_lists,
    ) = args
    width = KV * HEAD
    head_major = (
        queries.reshape(REQ, 2, KV, 8, HEAD).transpose(2, 0, 1, 3, 4).reshape(KV, ROWS, HEAD)
    )
    root_rows = root_keys.shape[0]
    bf16, f32 = jnp.bfloat16, jnp.float32
    vmem = pl.BlockSpec(memory_space=pltpu.VMEM)
    smem = pl.BlockSpec(memory_space=pltpu.SMEM)
    anywhere = pl.BlockSpec(memory_space=pl.ANY)
    dma = pltpu.SemaphoreType.DMA
    blocks = (nz, KV, ROWS, HEAD)
    out = pl.pallas_call(
        functools.partial(kernel, nz, ny),
        out_shape=jax.ShapeDtypeStruct((KV, ROWS, HEAD), bf16),
        in_specs=[vmem, vmem, vmem] + [anywhere] * 6 + [smem] * 4,
        out_specs=vmem,
        scratch_shapes=[
            pltpu.VMEM(blocks, bf16),
            pltpu.VMEM(blocks, bf16),
            pltpu.VMEM(blocks, bf16),
            pltpu.VMEM(blocks, bf16),
            pltpu.VMEM(blocks, bf16),
            pltpu.VMEM(blocks, bf16),
            pltpu.VMEM(blocks, bf16),
            pltpu.VMEM((2 * ny, 2, root_rows, width), bf16),
            pltpu.VMEM((2 * BLK, width), bf16),
            pltpu.VMEM((2 * BLK, width), bf16),
            pltpu.VMEM((LOCAL, width), bf16),
            pltpu.VMEM((LOCAL, width), bf16),
            pltpu.VMEM((nz, 2, ROWS), jnp.int32),
            pltpu.VMEM((NX, nz, 2, ROWS), jnp.int32),
            pltpu.VMEM((nz, ROWS, ROWS), bf16),
            pltpu.VMEM((nz, ROWS, ROWS), f32),
            pltpu.VMEM((nz, ROWS, HEAD), bf16),
            pltpu.VMEM((2 * BLK, HEAD), bf16),
            pltpu.VMEM((LOCAL, HEAD), bf16),
            pltpu.VMEM((ROWS, HEAD), bf16),
            pltpu.VMEM((nz, 2, KV, ROWS), f32),
            pltpu.VMEM((nz, 2, NX, KV, ROWS), f32),
            pltpu.VMEM((nz, 2, KV, ROWS), f32),
            pltpu.VMEM((nz, 2, KV, ROWS), f32),
            pltpu.VMEM((nz, 2, KV, ROWS), f32),
            pltpu.VMEM((KV, ROWS, HEAD), f32),
            pltpu.VMEM((KV, ROWS, HEAD), f32),
            pltpu.VMEM((KV, ROWS, HEAD), f32),
            pltpu.VMEM((2, ROWS, ROWS), f32),
            pltpu.VMEM((nz, ROWS, ROWS), f32),
            pltpu.VMEM((2 * ROWS, BLK), f32),
            pltpu.VMEM((2 * ROWS, BLK), f32),
            dma((6,)),
            dma((10,)),
            dma((3,)),
            dma((nz, 2)),
            dma((nz, 2)),
            dma((nz, 2)),
            dma((nz, 2)),
            dma((nz, 2)),
            dma((nz, 2)),
            dma((ny, 2)),
        ],
        compiler_params=pltpu.CompilerParams(
            collective_id=0, has_side_effects=True, vmem_limit_bytes=60 * 1024 * 1024 + 512 * 1024
        ),
        cost_estimate=pl.CostEstimate(
            flops=4_000_000_000, bytes_accessed=5_000_000, transcendentals=8_000_000
        ),
        name="shared_prefix_attention",
    )(
        head_major,
        new_keys,
        new_values,
        suffix_keys.reshape(REQ * SUF, width),
        suffix_values.reshape(REQ * SUF, width),
        root_keys,
        root_values,
        prefix_keys.reshape(2 * BLK, width),
        prefix_values.reshape(2 * BLK, width),
        suffix_lengths,
        prefix_lengths,
        owner_map,
        block_lists.T,
    )
    return out.reshape(KV, REQ, 2, 8, HEAD).transpose(1, 2, 0, 3, 4).reshape(REQ, 2, 64 * HEAD)


def solution(mesh):
    return jax.shard_map(
        functools.partial(shards, mesh.shape["dev"] // NX, mesh.shape["group"] // CORES),
        mesh=mesh,
        in_specs=(
            P(("group", "dev"), None, None),
            P(("group", "dev"), None, None),
            P(("group", "dev"), None, None),
            P(("group", "dev"), None, None),
            P(("group", "dev"), None, None),
            P(("group", "dev")),
            P("group", None),
            P("group", None),
            P(("group", "dev"), None, None),
            P(("group", "dev"), None, None),
            P(("group", "dev")),
            P("group", None),
            P(("group", "dev"), None),
        ),
        out_specs=P(("group", "dev"), None, None),
        check_vma=False,
    )
```

```python
import functools
import math

import jax
import jax.numpy as jnp
from jax import lax
from jax.experimental import pallas as pl
from jax.experimental.pallas import tpu as pltpu
from jax.sharding import PartitionSpec as P

KV = 8
HEAD = 128
NX = 4
CORES = 2
REQ = 8
ROWS = 128
SLOT_ROWS = 32
BLK = 256
SUF = 32
LOCAL = 384
HALF = KV // 2
FLOOR = -1.0e30
DROP = -2.0e30
SCALE = 1.0 / math.sqrt(HEAD)
LOG2E = 1.0 / math.log(2.0)
SCALE2 = SCALE * LOG2E
MESH = pl.DeviceIdType.MESH
NT = (((1,), (1,)), ((), ()))


def iota(shape, dim):
    return lax.broadcasted_iota(jnp.int32, shape, dim)


def kernel(
    nz,
    ny,
    q_ref,
    nk_ref,
    nv_ref,
    sk_ref,
    sv_ref,
    rk_ref,
    rv_ref,
    pk_ref,
    pv_ref,
    slen_ref,
    plen_ref,
    om_ref,
    bl_ref,
    out_ref,
    zq,
    snd,
    rcv,
    ans,
    ret,
    rsin,
    rsout,
    rkv,
    pk,
    pv,
    sk,
    sv,
    metaz,
    metax,
    onehot,
    bias_t,
    pick,
    kbias,
    lbias,
    lpick,
    lmine,
    lret,
    lslot,
    lin,
    lout,
    loc_acc,
    loc_max,
    loc_tot,
    lacc,
    second_slot,
    score_even,
    score_odd,
    local_sem,
    sent_sem,
    all_sem,
    zr_sem,
    xr_sem,
    br_sem,
    lr_sem,
    rr_sem,
    er_sem,
    yr_sem,
):
    zh = nz // 2
    yh = ny // 2
    group = lax.axis_index("group")
    dev = lax.axis_index("dev")
    z, x = dev // NX, dev % NX
    y, core = group // CORES, group % CORES

    def at_z(step):
        return (group, lax.rem(z + step + nz, nz) * NX + x)

    def at_x(step):
        return (group, z * NX + lax.rem(x + step, NX))

    def at_y(step):
        return (lax.rem(y + step + ny, ny) * CORES + core, dev)

    sibling = (y * CORES + 1 - core, dev)

    def send(src, dst, send_sem, recv_sem, device):
        pltpu.make_async_remote_copy(
            src_ref=src,
            dst_ref=dst,
            send_sem=send_sem,
            recv_sem=recv_sem,
            device_id=device,
            device_id_type=MESH,
        ).start()

    def arrived(ref, recv_sem):
        pltpu.make_async_copy(ref, ref, recv_sem).wait()

    loads = [
        pltpu.make_async_copy(rk_ref, rkv.at[0, 0], local_sem.at[0]),
        pltpu.make_async_copy(rv_ref, rkv.at[0, 1], local_sem.at[1]),
        pltpu.make_async_copy(pk_ref, pk, local_sem.at[2]),
        pltpu.make_async_copy(pv_ref, pv, local_sem.at[3]),
        pltpu.make_async_copy(sk_ref, sk.at[pl.ds(0, REQ * SUF)], local_sem.at[4]),
        pltpu.make_async_copy(sv_ref, sv.at[pl.ds(0, REQ * SUF)], local_sem.at[5]),
    ]
    for load in loads:
        load.start()

    partners = [at_z(step) for step in range(1, nz)]
    partners += [at_x(step) for step in range(1, NX)]
    if ny > 1:
        partners += [at_y(1), at_y(-1)]
    partners += [sibling]
    barrier = pltpu.get_barrier_semaphore()
    for partner in partners:
        pl.semaphore_signal(barrier, inc=1, device_id=partner, device_id_type=MESH)

    lane1 = iota((1, ROWS), 1)
    stored = [om_ref[0, bl_ref[p % 2, p // 2]] for p in range(2 * REQ)]
    owner = [s // 2 for s in stored]
    code_rows = [jnp.zeros((1, ROWS), jnp.int32), jnp.zeros((1, ROWS), jnp.int32)]
    for p in range(2 * REQ):
        rank = jnp.int32(0)
        for other in range(p):
            rank = rank + (owner[other] == owner[p]).astype(jnp.int32)
        code = owner[p] * 4 + rank * 2 + stored[p] % 2
        code_rows[p % 2] = jnp.where(lane1 // 16 == p // 2, code, code_rows[p % 2])
    metaz[0, pl.ds(0, 1), :] = code_rows[0]
    metaz[0, pl.ds(1, 1), :] = code_rows[1]

    pl.semaphore_wait(barrier, len(partners))

    def q_half(b, h):
        rows = pl.ds(h * HALF, HALF)
        return q_ref.at[rows] if b == 0 else zq.at[b, rows]

    def pass_queries(b, h, step, into):
        send(
            q_half(b, h),
            zq.at[into, pl.ds(h * HALF, HALF)],
            sent_sem.at[0],
            zr_sem.at[into, h],
            at_z(step),
        )

    def forward_queries(b, h):
        for step in (1, -1):
            if b == 0 or (step == 1) == (b > zh):
                if b == zh:
                    continue
                into = (b - step) % nz
                if into == zh and h != (0 if step == 1 else 1):
                    continue
                pass_queries(b, h, step, into)

    def query_arrived(b, h):
        arrived(zq.at[b, pl.ds(h * HALF, HALF)], zr_sem.at[b, h])

    for step in range(1, nz):
        send(
            metaz.at[0],
            metaz.at[(-step) % nz],
            sent_sem.at[1],
            all_sem.at[0],
            at_z(step),
        )

    for h in range(2):
        forward_queries(0, h)

    loads[0].wait()
    loads[1].wait()

    def share_root(b):
        send(rkv.at[b], rkv.at[ny + b], sent_sem.at[2], all_sem.at[1], sibling)

    def forward_root(b):
        for step in (1, -1):
            if b == 0 or (step == 1) == (b > yh):
                if b == yh or ny == 1:
                    continue
                into = (b - step) % ny
                if into == yh:
                    part = 0 if step == 1 else 1
                    send(
                        rkv.at[b, part],
                        rkv.at[into, part],
                        sent_sem.at[3],
                        yr_sem.at[into, part],
                        at_y(step),
                    )
                else:
                    send(
                        rkv.at[b],
                        rkv.at[into],
                        sent_sem.at[3],
                        yr_sem.at[into, 0],
                        at_y(step),
                    )

    def root_arrived(b):
        if b == yh:
            for part in range(2):
                arrived(rkv.at[b, part], yr_sem.at[b, part])
        else:
            arrived(rkv.at[b], yr_sem.at[b, 0])

    forward_root(0)
    share_root(0)

    row = iota((ROWS, ROWS), 0)
    lane = iota((ROWS, ROWS), 1)
    same_place = row % 16 == lane % 16
    diagonal = jnp.where(row == lane, 0.0, DROP)

    def there(step):
        return pl.ds(pl.multiple_of(lax.rem(x + step, NX) * SLOT_ROWS, SLOT_ROWS), SLOT_ROWS)

    mine = there(0)
    others = pl.ds(0, (NX - 1) * SLOT_ROWS)

    def route(b):
        wanted = z * (2 * NX) + row // 16
        first = metaz[b, pl.ds(0, 1), :] // 2
        second = metaz[b, pl.ds(1, 1), :] // 2
        hit = ((first == wanted) | (second == wanted)) & same_place
        onehot[b] = jnp.where(hit, 1.0, 0.0).astype(jnp.bfloat16)
        bias_t[b] = jnp.where(hit, 0.0, DROP).T

    def select(b, h):
        part = pl.ds(h * HALF, HALF)

        def body(k, carry):
            block = q_ref[k] if b == 0 else zq[b, k]
            chosen = jnp.dot(onehot[b], block, preferred_element_type=jnp.float32)
            snd[b, k] = chosen.astype(jnp.bfloat16)
            return carry

        lax.fori_loop(h * HALF, (h + 1) * HALF, body, 0, unroll=True)
        for step in range(1, NX):
            send(
                snd.at[b, part, there(step), :],
                rcv.at[b, part, mine, :],
                sent_sem.at[4],
                xr_sem.at[b, h],
                at_x(step),
            )

        def keep(k, carry):
            rcv[b, k, mine, :] = snd[b, k, mine, :]
            return carry

        lax.fori_loop(h * HALF, (h + 1) * HALF, keep, 0, unroll=True)

    def slots_arrived(b, h):
        arrived(rcv.at[b, pl.ds(h * HALF, HALF), others, :], xr_sem.at[b, h])

    ones_prefix = jnp.ones((BLK, HEAD), jnp.bfloat16)

    def label_slots(b):
        for source in range(NX):
            code = metax[source, b]
            srow = iota((SLOT_ROWS, ROWS), 0)
            slane = iota((SLOT_ROWS, ROWS), 1)
            wanted = (dev * 2 + srow // 16) * 2 + 1
            hit = (code[0:1, :] == wanted) | (code[1:2, :] == wanted)
            second = jnp.max(jnp.where(hit, 1.0, 0.0), axis=1, keepdims=True)
            here = pl.ds(source * SLOT_ROWS, SLOT_ROWS)
            pick[b, here, :] = jnp.where(
                slane == 0, 1.0 - second, jnp.where(slane == 1, second, 0.0)
            ).astype(jnp.bfloat16)
            second_slot[b, here, :] = jnp.broadcast_to(second, (SLOT_ROWS, ROWS))

    def serve(blocks, halves):
        rows = len(blocks) * ROWS
        last = HALF * (halves[-1] + 1) - 1

        def score(k, into):
            cols = pl.ds(pl.multiple_of(k * HEAD, HEAD), HEAD)
            queries = jnp.concatenate(
                [jnp.concatenate([rcv[b, k], pick[b]], axis=1) for b in blocks], axis=0
            )
            keys = jnp.concatenate([pk[:, cols], kbias[...]], axis=1)
            both = lax.dot_general(queries, keys, NT, preferred_element_type=jnp.float32)
            into[pl.ds(0, rows), :] = jnp.maximum(both[:, :BLK], both[:, BLK:])

        def weigh(k, source):
            cols = pl.ds(pl.multiple_of(k * HEAD, HEAD), HEAD)
            scores = source[pl.ds(0, rows), :]
            highest = jnp.max(scores, axis=1, keepdims=True)
            weights = jnp.exp2((scores - highest) * SCALE2).astype(jnp.bfloat16)
            values = jnp.concatenate([pv[:BLK, cols], pv[BLK:, cols], ones_prefix], axis=1)
            summed = jnp.dot(weights, values, preferred_element_type=jnp.float32)
            totals = summed[:, 2 * HEAD :]
            inverse = 1.0 / totals
            logs = highest * SCALE2 + jnp.log(totals) * LOG2E
            for at, b in enumerate(blocks):
                part = slice(at * ROWS, (at + 1) * ROWS)
                chosen = jnp.where(
                    second_slot[b] > 0.5, summed[part, HEAD : 2 * HEAD], summed[part, :HEAD]
                )
                ans[b, k] = (chosen * inverse[part]).astype(jnp.bfloat16)
                lacc[at] = jnp.where(lane == k, logs[part], lacc[at])

        def body(turn, carry):
            k = HALF * halves[0] + 2 * turn
            score(k + 1, score_odd)
            weigh(k, score_even)
            score(jnp.minimum(k + 2, last), score_even)
            weigh(k + 1, score_odd)
            return carry

        score(HALF * halves[0], score_even)
        lax.fori_loop(0, len(halves) * HALF // 2, body, 0)
        for at, b in enumerate(blocks):
            logs = lacc[at].T[:KV, :]
            for h in halves:
                lmine[b, h] = logs

    def give_back(b, h):
        part = pl.ds(h * HALF, HALF)
        for step in range(1, NX):
            send(
                ans.at[b, part, there(step), :],
                ret.at[b, part, mine, :],
                sent_sem.at[5],
                br_sem.at[b, h],
                at_x(step),
            )
            send(
                lmine.at[b, h],
                lret.at[b, h, NX - step],
                sent_sem.at[6],
                lr_sem.at[b, h],
                at_x(step),
            )

        def body(k, carry):
            ret[b, k, mine, :] = ans[b, k, mine, :]
            return carry

        lax.fori_loop(h * HALF, (h + 1) * HALF, body, 0, unroll=True)

    def answers_arrived(b, h):
        lane8 = iota((KV, ROWS), 1)
        rows = lmine[b, h]
        arrived(ret.at[b, pl.ds(h * HALF, HALF), others, :], br_sem.at[b, h])
        arrived(lret.at[b, h, pl.ds(1, NX - 1)], lr_sem.at[b, h])
        for step in range(1, NX):
            moved = pltpu.roll(lret[b, h, step], SLOT_ROWS * step, 1)
            rows = jnp.where(lane8 // SLOT_ROWS == lax.rem(x + step, NX), moved, rows)
        lslot[b, h] = rows

    def chain(b, h):
        step = 1 if b < zh or (b == zh and h == 0) else -1
        into = (b - step) % nz
        place = into if into else (0 if step == 1 else zh)
        return step, place

    def has_input(b, h):
        return b != zh and (b not in (zh - 1, zh + 1) or chain(zh, h)[1] == b)

    def partial_arrived(place, h):
        arrived(rsin.at[place, pl.ds(h * HALF, HALF)], rr_sem.at[place, h])
        arrived(lin.at[place, h], er_sem.at[place, h])

    def combine(blocks, h):
        for b in blocks:
            if has_input(b, h):
                partial_arrived(b, h)

        def body(k, carry):
            def logs(b):
                rows = jnp.broadcast_to(lslot[b, h, pl.ds(k, 1), :], (ROWS, ROWS)) + bias_t[b]
                if has_input(b, h):
                    extra = jnp.broadcast_to(lin[b, h, pl.ds(k, 1), :], (ROWS, ROWS)) + diagonal
                    rows = jnp.concatenate([rows, extra], axis=1)
                return rows

            highest = [
                jnp.maximum(jnp.max(logs(b), axis=1, keepdims=True), FLOOR) for b in blocks
            ]
            weights = [jnp.exp2(logs(b) - top).astype(jnp.bfloat16) for b, top in zip(blocks, highest)]
            sums = []
            for b, weight in zip(blocks, weights):
                parts = ret[b, k]
                if has_input(b, h):
                    parts = jnp.concatenate([parts, rsin[b, k]], axis=0)
                parts = jnp.concatenate([parts, jnp.ones_like(parts)], axis=1)
                sums.append(jnp.dot(weight, parts, preferred_element_type=jnp.float32))
            for at, b in enumerate(blocks):
                totals = jnp.maximum(sums[at][:, HEAD:], 1.0e-30)
                rsout[b, k] = (sums[at][:, :HEAD] / totals).astype(jnp.bfloat16)
                lacc[at] = jnp.where(lane == k, highest[at] + jnp.log(totals) * LOG2E, lacc[at])
            return carry

        lax.fori_loop(h * HALF, (h + 1) * HALF, body, 0, unroll=2)
        for at, b in enumerate(blocks):
            lout[b, h] = lacc[at].T[:KV, :]
            step, place = chain(b, h)
            part = pl.ds(h * HALF, HALF)
            send(
                rsout.at[b, part],
                rsin.at[place, part],
                sent_sem.at[7],
                rr_sem.at[place, h],
                at_z(step),
            )
            send(
                lout.at[b, h],
                lin.at[place, h],
                sent_sem.at[8],
                er_sem.at[place, h],
                at_z(step),
            )

    ones_root = jnp.ones((ny * CORES * rkv.shape[2], HEAD), jnp.bfloat16)
    ones_local = jnp.ones((LOCAL, HEAD), jnp.bfloat16)
    root_rows = ny * CORES * rkv.shape[2]

    def attend_local(k_from, k_to):
        def body(k, carry):
            cols = pl.ds(pl.multiple_of(k * HEAD, HEAD), HEAD)
            queries = q_ref[k]
            root_keys = rkv[:, 0, :, cols].reshape(root_rows, HEAD)
            root_values = rkv[:, 1, :, cols].reshape(root_rows, HEAD)
            root_scores = lax.dot_general(
                queries, root_keys, NT, preferred_element_type=jnp.float32
            )
            wide = jnp.concatenate([queries, lpick[...]], axis=1)
            keys = jnp.concatenate([sk[:, cols], lbias[...]], axis=1)
            scores = lax.dot_general(wide, keys, NT, preferred_element_type=jnp.float32)
            highest = jnp.maximum(
                jnp.max(root_scores, axis=1, keepdims=True),
                jnp.max(scores, axis=1, keepdims=True),
            )
            root_weights = jnp.exp2((root_scores - highest) * SCALE2).astype(jnp.bfloat16)
            weights = jnp.exp2((scores - highest) * SCALE2).astype(jnp.bfloat16)
            summed = jnp.dot(
                root_weights,
                jnp.concatenate([root_values, ones_root], axis=1),
                preferred_element_type=jnp.float32,
            ) + jnp.dot(
                weights,
                jnp.concatenate([sv[:, cols], ones_local], axis=1),
                preferred_element_type=jnp.float32,
            )
            loc_acc[k] = summed[:, :HEAD]
            loc_tot[k] = summed[:, HEAD:]
            loc_max[k] = jnp.broadcast_to(highest * SCALE2, (ROWS, ROWS))
            return carry

        lax.fori_loop(k_from, k_to, body, 0)

    def finish(h):
        partial_arrived(0, h)
        partial_arrived(zh, h)

        def body(k, carry):
            rows = jnp.concatenate(
                [
                    jnp.broadcast_to(lslot[0, h, pl.ds(k, 1), :], (ROWS, ROWS)) + bias_t[0],
                    jnp.broadcast_to(lin[0, h, pl.ds(k, 1), :], (ROWS, ROWS)) + diagonal,
                    jnp.broadcast_to(lin[zh, h, pl.ds(k, 1), :], (ROWS, ROWS)) + diagonal,
                ],
                axis=1,
            )
            highest = jnp.maximum(jnp.max(rows, axis=1, keepdims=True), loc_max[k])
            wide = jnp.concatenate([highest] * 3, axis=1)
            weights = jnp.exp2(rows - wide).astype(jnp.bfloat16)
            parts = jnp.concatenate([ret[0, k], rsin[0, k], rsin[zh, k]], axis=0)
            parts = jnp.concatenate([parts, jnp.ones_like(parts)], axis=1)
            summed = jnp.dot(weights, parts, preferred_element_type=jnp.float32)
            share = jnp.exp2(loc_max[k] - highest)
            numerator = summed[:, :HEAD] + loc_acc[k] * share
            denominator = summed[:, HEAD:] + loc_tot[k] * share
            out_ref[k] = (numerator / denominator).astype(jnp.bfloat16)
            return carry

        lax.fori_loop(h * HALF, (h + 1) * HALF, body, 0, unroll=2)

    lacc[...] = jnp.zeros_like(lacc)
    route(0)
    for h in range(2):
        select(0, h)

    prow = iota((2 * BLK, HEAD), 0)
    plane = iota((2 * BLK, HEAD), 1)
    limit = jnp.where(prow < BLK, plen_ref[0], plen_ref[1])
    live = prow % BLK < limit
    kbias[...] = jnp.where(
        (plane < 2) & ~((plane == prow // BLK) & live), DROP, 0.0
    ).astype(jnp.bfloat16)
    lrow = iota((LOCAL, HEAD), 0)
    llane = iota((LOCAL, HEAD), 1)
    length = jnp.zeros((LOCAL, HEAD), jnp.int32)
    for r in range(REQ):
        length = jnp.where(lrow // SUF == r, slen_ref[r], length)
    past = (lrow < REQ * SUF) & (llane // 2 == lrow // SUF) & (lrow % SUF < length)
    fresh_row = lrow - REQ * SUF
    fresh = (
        (fresh_row >= 0) & (llane // 2 == fresh_row // 16) & (fresh_row % 16 <= llane % 2)
    )
    lbias[...] = jnp.where((llane < 2 * REQ) & ~(past | fresh), DROP, 0.0).astype(jnp.bfloat16)
    lpick[...] = jnp.where(lane == row // 8, 1.0, 0.0).astype(jnp.bfloat16)
    for cache, new in ((sk, nk_ref), (sv, nv_ref)):
        cache[pl.ds(REQ * SUF, 16 * REQ), :] = jnp.zeros((16 * REQ, KV * HEAD), jnp.bfloat16)
        for r in range(REQ):
            cache[pl.ds(REQ * SUF + 16 * r, 2), :] = new[r]

    for load in loads[2:]:
        load.wait()
    def exchange_routes():
        arrived(metaz.at[pl.ds(1, nz - 1)], all_sem.at[0])
        for step in range(1, NX):
            send(
                metaz,
                metax.at[x],
                sent_sem.at[9],
                all_sem.at[2],
                at_x(step),
            )
        metax[x] = metaz[...]

    def advance_root(s):
        for b in (ny - s, s) if s < yh else (yh,):
            root_arrived(b)
            forward_root(b)
            share_root(b)

    def serve_step(s):
        blocks = (nz - s, s) if 0 < s < zh else (s,)
        for b in blocks:
            label_slots(b)
            for h in range(2):
                slots_arrived(b, h)
        serve(blocks, (0, 1))

    served = 0
    for s in range(1, zh + 1):
        blocks = (nz - s, s) if s < zh else (zh,)
        for h in range(2):
            for b in blocks:
                query_arrived(b, h)
                forward_queries(b, h)
        if s == 1:
            exchange_routes()
        for b in blocks:
            route(b)
        for h in range(2):
            for b in blocks:
                select(b, h)
        if s == min(2, zh):
            arrived(metax.at[pl.ds(0, NX - 1)], all_sem.at[2])
        while served < s - 1:
            serve_step(served)
            served += 1
        if s < min(zh, yh):
            advance_root(s)
        if s == zh - 1 and s > 1:
            serve_step(served)
            served += 1
    while served < zh:
        serve_step(served)
        served += 1
    label_slots(zh)

    order = [(zh,)] + [(s, nz - s) for s in range(zh - 1, 0, -1)] + [(0,)]
    for h in range(2):
        slots_arrived(zh, h)
        serve((zh,), (h,))
        give_back(zh, h)

    for s in range(min(zh, yh), yh + 1):
        advance_root(s)
    shares = [-(-KV * turn // (zh - 1)) for turn in range(zh)]
    for b in order[1]:
        give_back(b, 0)
    for turn, blocks in enumerate(order[:-1]):
        for h in range(2):
            for b in blocks:
                answers_arrived(b, h)
            if turn == 0:
                ahead = [(b, 1) for b in order[1]] if h == 0 else []
            else:
                ahead = [(b, h) for b in order[turn + 1]]
            for b, part in ahead:
                give_back(b, part)
            combine(blocks, h)
        if turn == 0:
            arrived(rkv.at[pl.ds(ny, ny)], all_sem.at[1])
        else:
            attend_local(shares[turn - 1], shares[turn])
    for h in range(2):
        answers_arrived(0, h)
        finish(h)

    for at, ref in enumerate(
        (
            zq.at[pl.ds(1, nz - 1)],
            metaz.at[pl.ds(1, nz - 1)],
            rkv.at[pl.ds(0, ny)],
            rkv.at[pl.ds(1, ny - 1)],
            rcv.at[:, :, others, :],
            ret.at[:, :, others, :],
            lret.at[:, :, pl.ds(1, NX - 1)],
            rsin.at[pl.ds(1, nz - 1)],
            lin.at[pl.ds(1, nz - 1)],
            metax.at[pl.ds(1, NX - 1)],
        )
    ):
        arrived(ref, sent_sem.at[at])


def shards(nz, ny, *args):
    (
        queries,
        new_keys,
        new_values,
        suffix_keys,
        suffix_values,
        suffix_lengths,
        root_keys,
        root_values,
        prefix_keys,
        prefix_values,
        prefix_lengths,
        owner_map,
        block_lists,
    ) = args
    width = KV * HEAD
    head_major = (
        queries.reshape(REQ, 2, KV, 8, HEAD).transpose(2, 0, 1, 3, 4).reshape(KV, ROWS, HEAD)
    )
    root_rows = root_keys.shape[0]
    bf16, f32 = jnp.bfloat16, jnp.float32
    vmem = pl.BlockSpec(memory_space=pltpu.VMEM)
    smem = pl.BlockSpec(memory_space=pltpu.SMEM)
    anywhere = pl.BlockSpec(memory_space=pl.ANY)
    dma = pltpu.SemaphoreType.DMA
    blocks = (nz, KV, ROWS, HEAD)
    out = pl.pallas_call(
        functools.partial(kernel, nz, ny),
        out_shape=jax.ShapeDtypeStruct((KV, ROWS, HEAD), bf16),
        in_specs=[vmem, vmem, vmem] + [anywhere] * 6 + [smem] * 4,
        out_specs=vmem,
        scratch_shapes=[
            pltpu.VMEM(blocks, bf16),
            pltpu.VMEM(blocks, bf16),
            pltpu.VMEM(blocks, bf16),
            pltpu.VMEM(blocks, bf16),
            pltpu.VMEM(blocks, bf16),
            pltpu.VMEM(blocks, bf16),
            pltpu.VMEM(blocks, bf16),
            pltpu.VMEM((2 * ny, 2, root_rows, width), bf16),
            pltpu.VMEM((2 * BLK, width), bf16),
            pltpu.VMEM((2 * BLK, width), bf16),
            pltpu.VMEM((LOCAL, width), bf16),
            pltpu.VMEM((LOCAL, width), bf16),
            pltpu.VMEM((nz, 2, ROWS), jnp.int32),
            pltpu.VMEM((NX, nz, 2, ROWS), jnp.int32),
            pltpu.VMEM((nz, ROWS, ROWS), bf16),
            pltpu.VMEM((nz, ROWS, ROWS), f32),
            pltpu.VMEM((nz, ROWS, HEAD), bf16),
            pltpu.VMEM((2 * BLK, HEAD), bf16),
            pltpu.VMEM((LOCAL, HEAD), bf16),
            pltpu.VMEM((ROWS, HEAD), bf16),
            pltpu.VMEM((nz, 2, KV, ROWS), f32),
            pltpu.VMEM((nz, 2, NX, KV, ROWS), f32),
            pltpu.VMEM((nz, 2, KV, ROWS), f32),
            pltpu.VMEM((nz, 2, KV, ROWS), f32),
            pltpu.VMEM((nz, 2, KV, ROWS), f32),
            pltpu.VMEM((KV, ROWS, HEAD), f32),
            pltpu.VMEM((KV, ROWS, HEAD), f32),
            pltpu.VMEM((KV, ROWS, HEAD), f32),
            pltpu.VMEM((2, ROWS, ROWS), f32),
            pltpu.VMEM((nz, ROWS, ROWS), f32),
            pltpu.VMEM((2 * ROWS, BLK), f32),
            pltpu.VMEM((2 * ROWS, BLK), f32),
            dma((6,)),
            dma((10,)),
            dma((3,)),
            dma((nz, 2)),
            dma((nz, 2)),
            dma((nz, 2)),
            dma((nz, 2)),
            dma((nz, 2)),
            dma((nz, 2)),
            dma((ny, 2)),
        ],
        compiler_params=pltpu.CompilerParams(
            collective_id=0, has_side_effects=True, vmem_limit_bytes=60 * 1024 * 1024 + 512 * 1024
        ),
        cost_estimate=pl.CostEstimate(
            flops=4_000_000_000, bytes_accessed=5_000_000, transcendentals=8_000_000
        ),
        name="shared_prefix_attention",
    )(
        head_major,
        new_keys,
        new_values,
        suffix_keys.reshape(REQ * SUF, width),
        suffix_values.reshape(REQ * SUF, width),
        root_keys,
        root_values,
        prefix_keys.reshape(2 * BLK, width),
        prefix_values.reshape(2 * BLK, width),
        suffix_lengths,
        prefix_lengths,
        owner_map,
        block_lists.T,
    )
    return out.reshape(KV, REQ, 2, 8, HEAD).transpose(1, 2, 0, 3, 4).reshape(REQ, 2, 64 * HEAD)


def solution(mesh):
    return jax.shard_map(
        functools.partial(shards, mesh.shape["dev"] // NX, mesh.shape["group"] // CORES),
        mesh=mesh,
        in_specs=(
            P(("group", "dev"), None, None),
            P(("group", "dev"), None, None),
            P(("group", "dev"), None, None),
            P(("group", "dev"), None, None),
            P(("group", "dev"), None, None),
            P(("group", "dev")),
            P("group", None),
            P("group", None),
            P(("group", "dev"), None, None),
            P(("group", "dev"), None, None),
            P(("group", "dev")),
            P("group", None),
            P(("group", "dev"), None),
        ),
        out_specs=P(("group", "dev"), None, None),
        check_vma=False,
    )
```

```python
import functools
import math

import jax
import jax.numpy as jnp
from jax import lax
from jax.experimental import pallas as pl
from jax.experimental.pallas import tpu as pltpu
from jax.sharding import PartitionSpec as P

KV = 8
HEAD = 128
NX = 4
CORES = 2
REQ = 8
ROWS = 128
SLOT_ROWS = 32
BLK = 256
SUF = 32
LOCAL = 384
HALF = KV // 2
FLOOR = -1.0e30
DROP = -2.0e30
SCALE = 1.0 / math.sqrt(HEAD)
LOG2E = 1.0 / math.log(2.0)
SCALE2 = SCALE * LOG2E
MESH = pl.DeviceIdType.MESH
NT = (((1,), (1,)), ((), ()))


def iota(shape, dim):
    return lax.broadcasted_iota(jnp.int32, shape, dim)


def kernel(
    nz,
    ny,
    q_in,
    nk_ref,
    nv_ref,
    sk_ref,
    sv_ref,
    rk_ref,
    rv_ref,
    pk_ref,
    pv_ref,
    slen_ref,
    plen_ref,
    om_ref,
    bl_ref,
    out_ref,
    q_ref,
    zq,
    snd,
    rcv,
    ans,
    ret,
    rsin,
    rsout,
    rkv,
    pk,
    pv,
    sk,
    sv,
    metaz,
    metax,
    onehot,
    bias_t,
    pick,
    kbias,
    lbias,
    lpick,
    lmine,
    lret,
    lslot,
    lin,
    lout,
    loc_acc,
    loc_max,
    loc_tot,
    lacc,
    second_slot,
    score_even,
    score_odd,
    local_sem,
    sent_sem,
    all_sem,
    zr_sem,
    xr_sem,
    br_sem,
    lr_sem,
    rr_sem,
    er_sem,
    yr_sem,
):
    zh = nz // 2
    yh = ny // 2
    group = lax.axis_index("group")
    dev = lax.axis_index("dev")
    z, x = dev // NX, dev % NX
    y, core = group // CORES, group % CORES

    def at_z(step):
        return (group, lax.rem(z + step + nz, nz) * NX + x)

    def at_x(step):
        return (group, z * NX + lax.rem(x + step, NX))

    def at_y(step):
        return (lax.rem(y + step + ny, ny) * CORES + core, dev)

    sibling = (y * CORES + 1 - core, dev)

    def send(src, dst, send_sem, recv_sem, device):
        pltpu.make_async_remote_copy(
            src_ref=src,
            dst_ref=dst,
            send_sem=send_sem,
            recv_sem=recv_sem,
            device_id=device,
            device_id_type=MESH,
        ).start()

    def arrived(ref, recv_sem):
        pltpu.make_async_copy(ref, ref, recv_sem).wait()

    loads = [
        pltpu.make_async_copy(rk_ref, rkv.at[0, 0], local_sem.at[0]),
        pltpu.make_async_copy(rv_ref, rkv.at[0, 1], local_sem.at[1]),
        pltpu.make_async_copy(pk_ref, pk, local_sem.at[2]),
        pltpu.make_async_copy(pv_ref, pv, local_sem.at[3]),
        pltpu.make_async_copy(sk_ref, sk.at[pl.ds(0, REQ * SUF)], local_sem.at[4]),
        pltpu.make_async_copy(sv_ref, sv.at[pl.ds(0, REQ * SUF)], local_sem.at[5]),
    ]
    for load in loads:
        load.start()

    partners = [at_z(step) for step in range(1, nz)]
    partners += [at_x(step) for step in range(1, NX)]
    if ny > 1:
        partners += [at_y(1), at_y(-1)]
    partners += [sibling]
    barrier = pltpu.get_barrier_semaphore()
    for partner in partners:
        pl.semaphore_signal(barrier, inc=1, device_id=partner, device_id_type=MESH)

    for k in range(KV):
        q_ref[k] = q_in[:, :, k].reshape(ROWS, HEAD)

    lane1 = iota((1, ROWS), 1)
    stored = [om_ref[0, bl_ref[p % 2, p // 2]] for p in range(2 * REQ)]
    owner = [s // 2 for s in stored]
    code_rows = [jnp.zeros((1, ROWS), jnp.int32), jnp.zeros((1, ROWS), jnp.int32)]
    for p in range(2 * REQ):
        rank = jnp.int32(0)
        for other in range(p):
            rank = rank + (owner[other] == owner[p]).astype(jnp.int32)
        code = owner[p] * 4 + rank * 2 + stored[p] % 2
        code_rows[p % 2] = jnp.where(lane1 // 16 == p // 2, code, code_rows[p % 2])
    metaz[0, pl.ds(0, 1), :] = code_rows[0]
    metaz[0, pl.ds(1, 1), :] = code_rows[1]

    pl.semaphore_wait(barrier, len(partners))

    def q_half(b, h):
        rows = pl.ds(h * HALF, HALF)
        return q_ref.at[rows] if b == 0 else zq.at[b, rows]

    def pass_queries(b, h, step, into):
        send(
            q_half(b, h),
            zq.at[into, pl.ds(h * HALF, HALF)],
            sent_sem.at[0],
            zr_sem.at[into, h],
            at_z(step),
        )

    def forward_queries(b, h):
        for step in (1, -1):
            if b == 0 or (step == 1) == (b > zh):
                if b == zh:
                    continue
                into = (b - step) % nz
                if into == zh and h != (0 if step == 1 else 1):
                    continue
                pass_queries(b, h, step, into)

    def query_arrived(b, h):
        arrived(zq.at[b, pl.ds(h * HALF, HALF)], zr_sem.at[b, h])

    for step in range(1, nz):
        send(
            metaz.at[0],
            metaz.at[(-step) % nz],
            sent_sem.at[1],
            all_sem.at[0],
            at_z(step),
        )

    for h in range(2):
        forward_queries(0, h)

    loads[0].wait()
    loads[1].wait()

    def share_root(b):
        send(rkv.at[b], rkv.at[ny + b], sent_sem.at[2], all_sem.at[1], sibling)

    def forward_root(b):
        for step in (1, -1):
            if b == 0 or (step == 1) == (b > yh):
                if b == yh or ny == 1:
                    continue
                into = (b - step) % ny
                if into == yh:
                    part = 0 if step == 1 else 1
                    send(
                        rkv.at[b, part],
                        rkv.at[into, part],
                        sent_sem.at[3],
                        yr_sem.at[into, part],
                        at_y(step),
                    )
                else:
                    send(
                        rkv.at[b],
                        rkv.at[into],
                        sent_sem.at[3],
                        yr_sem.at[into, 0],
                        at_y(step),
                    )

    def root_arrived(b):
        if b == yh:
            for part in range(2):
                arrived(rkv.at[b, part], yr_sem.at[b, part])
        else:
            arrived(rkv.at[b], yr_sem.at[b, 0])

    forward_root(0)
    share_root(0)

    row = iota((ROWS, ROWS), 0)
    lane = iota((ROWS, ROWS), 1)
    same_place = row % 16 == lane % 16
    diagonal = jnp.where(row == lane, 0.0, DROP)

    def there(step):
        return pl.ds(pl.multiple_of(lax.rem(x + step, NX) * SLOT_ROWS, SLOT_ROWS), SLOT_ROWS)

    mine = there(0)
    others = pl.ds(0, (NX - 1) * SLOT_ROWS)

    def route(b):
        wanted = z * (2 * NX) + row // 16
        first = metaz[b, pl.ds(0, 1), :] // 2
        second = metaz[b, pl.ds(1, 1), :] // 2
        hit = ((first == wanted) | (second == wanted)) & same_place
        onehot[b] = jnp.where(hit, 1.0, 0.0).astype(jnp.bfloat16)
        bias_t[b] = jnp.where(hit, 0.0, DROP).T

    def select(b, h):
        part = pl.ds(h * HALF, HALF)

        def body(k, carry):
            block = q_ref[k] if b == 0 else zq[b, k]
            chosen = jnp.dot(onehot[b], block, preferred_element_type=jnp.float32)
            snd[b, k] = chosen.astype(jnp.bfloat16)
            return carry

        lax.fori_loop(h * HALF, (h + 1) * HALF, body, 0, unroll=True)
        for step in range(1, NX):
            send(
                snd.at[b, part, there(step), :],
                rcv.at[b, part, mine, :],
                sent_sem.at[4],
                xr_sem.at[b, h],
                at_x(step),
            )

        def keep(k, carry):
            rcv[b, k, mine, :] = snd[b, k, mine, :]
            return carry

        lax.fori_loop(h * HALF, (h + 1) * HALF, keep, 0, unroll=True)

    def slots_arrived(b, h):
        arrived(rcv.at[b, pl.ds(h * HALF, HALF), others, :], xr_sem.at[b, h])

    ones_prefix = jnp.ones((BLK, HEAD), jnp.bfloat16)

    def label_slots(b):
        for source in range(NX):
            code = metax[source, b]
            srow = iota((SLOT_ROWS, ROWS), 0)
            slane = iota((SLOT_ROWS, ROWS), 1)
            wanted = (dev * 2 + srow // 16) * 2 + 1
            hit = (code[0:1, :] == wanted) | (code[1:2, :] == wanted)
            second = jnp.max(jnp.where(hit, 1.0, 0.0), axis=1, keepdims=True)
            here = pl.ds(source * SLOT_ROWS, SLOT_ROWS)
            pick[b, here, :] = jnp.where(
                slane == 0, 1.0 - second, jnp.where(slane == 1, second, 0.0)
            ).astype(jnp.bfloat16)
            second_slot[b, here, :] = jnp.broadcast_to(second, (SLOT_ROWS, ROWS))

    def serve(blocks, halves):
        rows = len(blocks) * ROWS
        last = HALF * (halves[-1] + 1) - 1

        def score(k, into):
            cols = pl.ds(pl.multiple_of(k * HEAD, HEAD), HEAD)
            queries = jnp.concatenate(
                [jnp.concatenate([rcv[b, k], pick[b]], axis=1) for b in blocks], axis=0
            )
            keys = jnp.concatenate([pk[:, cols], kbias[...]], axis=1)
            both = lax.dot_general(queries, keys, NT, preferred_element_type=jnp.float32)
            into[pl.ds(0, rows), :] = jnp.maximum(both[:, :BLK], both[:, BLK:])

        def weigh(k, source):
            cols = pl.ds(pl.multiple_of(k * HEAD, HEAD), HEAD)
            scores = source[pl.ds(0, rows), :]
            highest = jnp.max(scores, axis=1, keepdims=True)
            weights = jnp.exp2((scores - highest) * SCALE2).astype(jnp.bfloat16)
            values = jnp.concatenate([pv[:BLK, cols], pv[BLK:, cols], ones_prefix], axis=1)
            summed = jnp.dot(weights, values, preferred_element_type=jnp.float32)
            totals = summed[:, 2 * HEAD :]
            inverse = 1.0 / totals
            logs = highest * SCALE2 + jnp.log(totals) * LOG2E
            for at, b in enumerate(blocks):
                part = slice(at * ROWS, (at + 1) * ROWS)
                chosen = jnp.where(
                    second_slot[b] > 0.5, summed[part, HEAD : 2 * HEAD], summed[part, :HEAD]
                )
                ans[b, k] = (chosen * inverse[part]).astype(jnp.bfloat16)
                lacc[at] = jnp.where(lane == k, logs[part], lacc[at])

        def body(turn, carry):
            k = HALF * halves[0] + 2 * turn
            score(k + 1, score_odd)
            weigh(k, score_even)
            score(jnp.minimum(k + 2, last), score_even)
            weigh(k + 1, score_odd)
            return carry

        score(HALF * halves[0], score_even)
        lax.fori_loop(0, len(halves) * HALF // 2, body, 0)
        for at, b in enumerate(blocks):
            logs = lacc[at].T[:KV, :]
            for h in halves:
                lmine[b, h] = logs

    def give_back(b, h):
        part = pl.ds(h * HALF, HALF)
        for step in range(1, NX):
            send(
                ans.at[b, part, there(step), :],
                ret.at[b, part, mine, :],
                sent_sem.at[5],
                br_sem.at[b, h],
                at_x(step),
            )
            send(
                lmine.at[b, h],
                lret.at[b, h, NX - step],
                sent_sem.at[6],
                lr_sem.at[b, h],
                at_x(step),
            )

        def body(k, carry):
            ret[b, k, mine, :] = ans[b, k, mine, :]
            return carry

        lax.fori_loop(h * HALF, (h + 1) * HALF, body, 0, unroll=True)

    def answers_arrived(b, h):
        lane8 = iota((KV, ROWS), 1)
        rows = lmine[b, h]
        arrived(ret.at[b, pl.ds(h * HALF, HALF), others, :], br_sem.at[b, h])
        arrived(lret.at[b, h, pl.ds(1, NX - 1)], lr_sem.at[b, h])
        for step in range(1, NX):
            moved = pltpu.roll(lret[b, h, step], SLOT_ROWS * step, 1)
            rows = jnp.where(lane8 // SLOT_ROWS == lax.rem(x + step, NX), moved, rows)
        lslot[b, h] = rows

    def chain(b, h):
        step = 1 if b < zh or (b == zh and h == 0) else -1
        into = (b - step) % nz
        place = into if into else (0 if step == 1 else zh)
        return step, place

    def has_input(b, h):
        return b != zh and (b not in (zh - 1, zh + 1) or chain(zh, h)[1] == b)

    def partial_arrived(place, h):
        arrived(rsin.at[place, pl.ds(h * HALF, HALF)], rr_sem.at[place, h])
        arrived(lin.at[place, h], er_sem.at[place, h])

    def combine(blocks, h):
        for b in blocks:
            if has_input(b, h):
                partial_arrived(b, h)

        def body(k, carry):
            def logs(b):
                rows = jnp.broadcast_to(lslot[b, h, pl.ds(k, 1), :], (ROWS, ROWS)) + bias_t[b]
                if has_input(b, h):
                    extra = jnp.broadcast_to(lin[b, h, pl.ds(k, 1), :], (ROWS, ROWS)) + diagonal
                    rows = jnp.concatenate([rows, extra], axis=1)
                return rows

            highest = [
                jnp.maximum(jnp.max(logs(b), axis=1, keepdims=True), FLOOR) for b in blocks
            ]
            weights = [jnp.exp2(logs(b) - top).astype(jnp.bfloat16) for b, top in zip(blocks, highest)]
            sums = []
            for b, weight in zip(blocks, weights):
                parts = ret[b, k]
                if has_input(b, h):
                    parts = jnp.concatenate([parts, rsin[b, k]], axis=0)
                parts = jnp.concatenate([parts, jnp.ones_like(parts)], axis=1)
                sums.append(jnp.dot(weight, parts, preferred_element_type=jnp.float32))
            for at, b in enumerate(blocks):
                totals = jnp.maximum(sums[at][:, HEAD:], 1.0e-30)
                rsout[b, k] = (sums[at][:, :HEAD] / totals).astype(jnp.bfloat16)
                lacc[at] = jnp.where(lane == k, highest[at] + jnp.log(totals) * LOG2E, lacc[at])
            return carry

        lax.fori_loop(h * HALF, (h + 1) * HALF, body, 0, unroll=2)
        for at, b in enumerate(blocks):
            lout[b, h] = lacc[at].T[:KV, :]
            step, place = chain(b, h)
            part = pl.ds(h * HALF, HALF)
            send(
                rsout.at[b, part],
                rsin.at[place, part],
                sent_sem.at[7],
                rr_sem.at[place, h],
                at_z(step),
            )
            send(
                lout.at[b, h],
                lin.at[place, h],
                sent_sem.at[8],
                er_sem.at[place, h],
                at_z(step),
            )

    ones_root = jnp.ones((ny * CORES * rkv.shape[2], HEAD), jnp.bfloat16)
    ones_local = jnp.ones((LOCAL, HEAD), jnp.bfloat16)
    root_rows = ny * CORES * rkv.shape[2]

    def attend_local(k_from, k_to):
        def body(k, carry):
            cols = pl.ds(pl.multiple_of(k * HEAD, HEAD), HEAD)
            queries = q_ref[k]
            root_keys = rkv[:, 0, :, cols].reshape(root_rows, HEAD)
            root_values = rkv[:, 1, :, cols].reshape(root_rows, HEAD)
            root_scores = lax.dot_general(
                queries, root_keys, NT, preferred_element_type=jnp.float32
            )
            wide = jnp.concatenate([queries, lpick[...]], axis=1)
            keys = jnp.concatenate([sk[:, cols], lbias[...]], axis=1)
            scores = lax.dot_general(wide, keys, NT, preferred_element_type=jnp.float32)
            highest = jnp.maximum(
                jnp.max(root_scores, axis=1, keepdims=True),
                jnp.max(scores, axis=1, keepdims=True),
            )
            root_weights = jnp.exp2((root_scores - highest) * SCALE2).astype(jnp.bfloat16)
            weights = jnp.exp2((scores - highest) * SCALE2).astype(jnp.bfloat16)
            summed = jnp.dot(
                root_weights,
                jnp.concatenate([root_values, ones_root], axis=1),
                preferred_element_type=jnp.float32,
            ) + jnp.dot(
                weights,
                jnp.concatenate([sv[:, cols], ones_local], axis=1),
                preferred_element_type=jnp.float32,
            )
            loc_acc[k] = summed[:, :HEAD]
            loc_tot[k] = summed[:, HEAD:]
            loc_max[k] = jnp.broadcast_to(highest * SCALE2, (ROWS, ROWS))
            return carry

        lax.fori_loop(k_from, k_to, body, 0)

    def finish(h):
        partial_arrived(0, h)
        partial_arrived(zh, h)

        def body(k, carry):
            rows = jnp.concatenate(
                [
                    jnp.broadcast_to(lslot[0, h, pl.ds(k, 1), :], (ROWS, ROWS)) + bias_t[0],
                    jnp.broadcast_to(lin[0, h, pl.ds(k, 1), :], (ROWS, ROWS)) + diagonal,
                    jnp.broadcast_to(lin[zh, h, pl.ds(k, 1), :], (ROWS, ROWS)) + diagonal,
                ],
                axis=1,
            )
            highest = jnp.maximum(jnp.max(rows, axis=1, keepdims=True), loc_max[k])
            wide = jnp.concatenate([highest] * 3, axis=1)
            weights = jnp.exp2(rows - wide).astype(jnp.bfloat16)
            parts = jnp.concatenate([ret[0, k], rsin[0, k], rsin[zh, k]], axis=0)
            parts = jnp.concatenate([parts, jnp.ones_like(parts)], axis=1)
            summed = jnp.dot(weights, parts, preferred_element_type=jnp.float32)
            share = jnp.exp2(loc_max[k] - highest)
            numerator = summed[:, :HEAD] + loc_acc[k] * share
            denominator = summed[:, HEAD:] + loc_tot[k] * share
            out_ref[:, :, k] = (
                (numerator / denominator).astype(jnp.bfloat16).reshape(REQ, 2, KV, HEAD)
            )
            return carry

        lax.fori_loop(h * HALF, (h + 1) * HALF, body, 0, unroll=2)

    lacc[...] = jnp.zeros_like(lacc)
    route(0)
    for h in range(2):
        select(0, h)

    prow = iota((2 * BLK, HEAD), 0)
    plane = iota((2 * BLK, HEAD), 1)
    limit = jnp.where(prow < BLK, plen_ref[0], plen_ref[1])
    live = prow % BLK < limit
    kbias[...] = jnp.where(
        (plane < 2) & ~((plane == prow // BLK) & live), DROP, 0.0
    ).astype(jnp.bfloat16)
    lrow = iota((LOCAL, HEAD), 0)
    llane = iota((LOCAL, HEAD), 1)
    length = jnp.zeros((LOCAL, HEAD), jnp.int32)
    for r in range(REQ):
        length = jnp.where(lrow // SUF == r, slen_ref[r], length)
    past = (lrow < REQ * SUF) & (llane // 2 == lrow // SUF) & (lrow % SUF < length)
    fresh_row = lrow - REQ * SUF
    fresh = (
        (fresh_row >= 0) & (llane // 2 == fresh_row // 16) & (fresh_row % 16 <= llane % 2)
    )
    lbias[...] = jnp.where((llane < 2 * REQ) & ~(past | fresh), DROP, 0.0).astype(jnp.bfloat16)
    lpick[...] = jnp.where(lane == row // 8, 1.0, 0.0).astype(jnp.bfloat16)
    for cache, new in ((sk, nk_ref), (sv, nv_ref)):
        cache[pl.ds(REQ * SUF, 16 * REQ), :] = jnp.zeros((16 * REQ, KV * HEAD), jnp.bfloat16)
        for r in range(REQ):
            cache[pl.ds(REQ * SUF + 16 * r, 2), :] = new[r]

    for load in loads[2:]:
        load.wait()
    def exchange_routes():
        arrived(metaz.at[pl.ds(1, nz - 1)], all_sem.at[0])
        for step in range(1, NX):
            send(
                metaz,
                metax.at[x],
                sent_sem.at[9],
                all_sem.at[2],
                at_x(step),
            )
        metax[x] = metaz[...]

    def advance_root(s):
        for b in (ny - s, s) if s < yh else (yh,):
            root_arrived(b)
            forward_root(b)
            share_root(b)

    def serve_step(s):
        blocks = (nz - s, s) if 0 < s < zh else (s,)
        for b in blocks:
            label_slots(b)
            for h in range(2):
                slots_arrived(b, h)
        serve(blocks, (0, 1))

    served = 0
    for s in range(1, zh + 1):
        blocks = (nz - s, s) if s < zh else (zh,)
        for h in range(2):
            for b in blocks:
                query_arrived(b, h)
                forward_queries(b, h)
        if s == 1:
            exchange_routes()
        for b in blocks:
            route(b)
        for h in range(2):
            for b in blocks:
                select(b, h)
        if s == min(2, zh):
            arrived(metax.at[pl.ds(0, NX - 1)], all_sem.at[2])
        while served < s - 1:
            serve_step(served)
            served += 1
        if s < min(zh, yh):
            advance_root(s)
        if s == zh - 1 and s > 1:
            serve_step(served)
            served += 1
    while served < zh:
        serve_step(served)
        served += 1
    label_slots(zh)

    order = [(zh,)] + [(s, nz - s) for s in range(zh - 1, 0, -1)] + [(0,)]
    for h in range(2):
        slots_arrived(zh, h)
        serve((zh,), (h,))
        give_back(zh, h)

    for s in range(min(zh, yh), yh + 1):
        advance_root(s)
    shares = [-(-KV * turn // (zh - 1)) for turn in range(zh)]
    for b in order[1]:
        give_back(b, 0)
    for turn, blocks in enumerate(order[:-1]):
        for h in range(2):
            for b in blocks:
                answers_arrived(b, h)
            if turn == 0:
                ahead = [(b, 1) for b in order[1]] if h == 0 else []
            else:
                ahead = [(b, h) for b in order[turn + 1]]
            combine(blocks, h)
            for b, part in ahead:
                give_back(b, part)
        if turn == 0:
            arrived(rkv.at[pl.ds(ny, ny)], all_sem.at[1])
        else:
            attend_local(shares[turn - 1], shares[turn])
    for h in range(2):
        answers_arrived(0, h)
        finish(h)

    for at, ref in enumerate(
        (
            zq.at[pl.ds(1, nz - 1)],
            metaz.at[pl.ds(1, nz - 1)],
            rkv.at[pl.ds(0, ny)],
            rkv.at[pl.ds(1, ny - 1)],
            rcv.at[:, :, others, :],
            ret.at[:, :, others, :],
            lret.at[:, :, pl.ds(1, NX - 1)],
            rsin.at[pl.ds(1, nz - 1)],
            lin.at[pl.ds(1, nz - 1)],
            metax.at[pl.ds(1, NX - 1)],
        )
    ):
        arrived(ref, sent_sem.at[at])


def shards(nz, ny, *args):
    (
        queries,
        new_keys,
        new_values,
        suffix_keys,
        suffix_values,
        suffix_lengths,
        root_keys,
        root_values,
        prefix_keys,
        prefix_values,
        prefix_lengths,
        owner_map,
        block_lists,
    ) = args
    width = KV * HEAD
    root_rows = root_keys.shape[0]
    bf16, f32 = jnp.bfloat16, jnp.float32
    vmem = pl.BlockSpec(memory_space=pltpu.VMEM)
    smem = pl.BlockSpec(memory_space=pltpu.SMEM)
    anywhere = pl.BlockSpec(memory_space=pl.ANY)
    dma = pltpu.SemaphoreType.DMA
    blocks = (nz, KV, ROWS, HEAD)
    out = pl.pallas_call(
        functools.partial(kernel, nz, ny),
        out_shape=jax.ShapeDtypeStruct((REQ, 2, KV, 8, HEAD), bf16),
        in_specs=[vmem, vmem, vmem] + [anywhere] * 6 + [smem] * 4,
        out_specs=vmem,
        scratch_shapes=[
            pltpu.VMEM(blocks[1:], bf16),
            pltpu.VMEM(blocks, bf16),
            pltpu.VMEM(blocks, bf16),
            pltpu.VMEM(blocks, bf16),
            pltpu.VMEM(blocks, bf16),
            pltpu.VMEM(blocks, bf16),
            pltpu.VMEM(blocks, bf16),
            pltpu.VMEM(blocks, bf16),
            pltpu.VMEM((2 * ny, 2, root_rows, width), bf16),
            pltpu.VMEM((2 * BLK, width), bf16),
            pltpu.VMEM((2 * BLK, width), bf16),
            pltpu.VMEM((LOCAL, width), bf16),
            pltpu.VMEM((LOCAL, width), bf16),
            pltpu.VMEM((nz, 2, ROWS), jnp.int32),
            pltpu.VMEM((NX, nz, 2, ROWS), jnp.int32),
            pltpu.VMEM((nz, ROWS, ROWS), bf16),
            pltpu.VMEM((nz, ROWS, ROWS), f32),
            pltpu.VMEM((nz, ROWS, HEAD), bf16),
            pltpu.VMEM((2 * BLK, HEAD), bf16),
            pltpu.VMEM((LOCAL, HEAD), bf16),
            pltpu.VMEM((ROWS, HEAD), bf16),
            pltpu.VMEM((nz, 2, KV, ROWS), f32),
            pltpu.VMEM((nz, 2, NX, KV, ROWS), f32),
            pltpu.VMEM((nz, 2, KV, ROWS), f32),
            pltpu.VMEM((nz, 2, KV, ROWS), f32),
            pltpu.VMEM((nz, 2, KV, ROWS), f32),
            pltpu.VMEM((KV, ROWS, HEAD), f32),
            pltpu.VMEM((KV, ROWS, HEAD), f32),
            pltpu.VMEM((KV, ROWS, HEAD), f32),
            pltpu.VMEM((2, ROWS, ROWS), f32),
            pltpu.VMEM((nz, ROWS, ROWS), f32),
            pltpu.VMEM((2 * ROWS, BLK), f32),
            pltpu.VMEM((2 * ROWS, BLK), f32),
            dma((6,)),
            dma((10,)),
            dma((3,)),
            dma((nz, 2)),
            dma((nz, 2)),
            dma((nz, 2)),
            dma((nz, 2)),
            dma((nz, 2)),
            dma((nz, 2)),
            dma((ny, 2)),
        ],
        compiler_params=pltpu.CompilerParams(
            collective_id=0, has_side_effects=True, vmem_limit_bytes=60 * 1024 * 1024 + 512 * 1024
        ),
        cost_estimate=pl.CostEstimate(
            flops=4_000_000_000, bytes_accessed=5_000_000, transcendentals=8_000_000
        ),
        name="shared_prefix_attention",
    )(
        queries.reshape(REQ, 2, KV, 8, HEAD),
        new_keys,
        new_values,
        suffix_keys.reshape(REQ * SUF, width),
        suffix_values.reshape(REQ * SUF, width),
        root_keys,
        root_values,
        prefix_keys.reshape(2 * BLK, width),
        prefix_values.reshape(2 * BLK, width),
        suffix_lengths,
        prefix_lengths,
        owner_map,
        block_lists.T,
    )
    return out.reshape(REQ, 2, 64 * HEAD)


def solution(mesh):
    return jax.shard_map(
        functools.partial(shards, mesh.shape["dev"] // NX, mesh.shape["group"] // CORES),
        mesh=mesh,
        in_specs=(
            P(("group", "dev"), None, None),
            P(("group", "dev"), None, None),
            P(("group", "dev"), None, None),
            P(("group", "dev"), None, None),
            P(("group", "dev"), None, None),
            P(("group", "dev")),
            P("group", None),
            P("group", None),
            P(("group", "dev"), None, None),
            P(("group", "dev"), None, None),
            P(("group", "dev")),
            P("group", None),
            P(("group", "dev"), None),
        ),
        out_specs=P(("group", "dev"), None, None),
        check_vma=False,
    )
```

```python
import functools
import math

import jax
import jax.numpy as jnp
from jax import lax
from jax.experimental import pallas as pl
from jax.experimental.pallas import tpu as pltpu
from jax.sharding import PartitionSpec as P

KV = 8
HEAD = 128
NX = 4
CORES = 2
REQ = 8
ROWS = 128
SLOT_ROWS = 32
BLK = 256
SUF = 32
LOCAL = 384
HALF = KV // 2
FLOOR = -1.0e30
DROP = -2.0e30
SCALE = 1.0 / math.sqrt(HEAD)
LOG2E = 1.0 / math.log(2.0)
SCALE2 = SCALE * LOG2E
MESH = pl.DeviceIdType.MESH
NT = (((1,), (1,)), ((), ()))


def iota(shape, dim):
    return lax.broadcasted_iota(jnp.int32, shape, dim)


def kernel(
    nz,
    ny,
    q_in,
    nk_ref,
    nv_ref,
    sk_ref,
    sv_ref,
    rk_ref,
    rv_ref,
    pk_ref,
    pv_ref,
    slen_ref,
    plen_ref,
    om_ref,
    bl_ref,
    out_ref,
    q_ref,
    zq,
    snd,
    rcv,
    ans,
    ret,
    rsin,
    rsout,
    rkv,
    pk,
    pv,
    sk,
    sv,
    metaz,
    metax,
    onehot,
    bias_t,
    pick,
    kbias,
    lbias,
    lpick,
    lmine,
    lret,
    lslot,
    lin,
    lout,
    loc_acc,
    loc_max,
    loc_tot,
    lacc,
    second_slot,
    score_even,
    score_odd,
    local_sem,
    sent_sem,
    all_sem,
    zr_sem,
    xr_sem,
    br_sem,
    lr_sem,
    rr_sem,
    er_sem,
    yr_sem,
):
    zh = nz // 2
    yh = ny // 2
    group = lax.axis_index("group")
    dev = lax.axis_index("dev")
    z, x = dev // NX, dev % NX
    y, core = group // CORES, group % CORES

    def at_z(step):
        return (group, lax.rem(z + step + nz, nz) * NX + x)

    def at_x(step):
        return (group, z * NX + lax.rem(x + step, NX))

    def at_y(step):
        return (lax.rem(y + step + ny, ny) * CORES + core, dev)

    sibling = (y * CORES + 1 - core, dev)

    def send(src, dst, send_sem, recv_sem, device):
        pltpu.make_async_remote_copy(
            src_ref=src,
            dst_ref=dst,
            send_sem=send_sem,
            recv_sem=recv_sem,
            device_id=device,
            device_id_type=MESH,
        ).start()

    def arrived(ref, recv_sem):
        pltpu.make_async_copy(ref, ref, recv_sem).wait()

    loads = [
        pltpu.make_async_copy(rk_ref, rkv.at[0, 0], local_sem.at[0]),
        pltpu.make_async_copy(rv_ref, rkv.at[0, 1], local_sem.at[1]),
        pltpu.make_async_copy(pk_ref, pk, local_sem.at[2]),
        pltpu.make_async_copy(pv_ref, pv, local_sem.at[3]),
        pltpu.make_async_copy(sk_ref, sk.at[pl.ds(0, REQ * SUF)], local_sem.at[4]),
        pltpu.make_async_copy(sv_ref, sv.at[pl.ds(0, REQ * SUF)], local_sem.at[5]),
    ]
    for load in loads:
        load.start()

    partners = [at_z(step) for step in range(1, nz)]
    partners += [at_x(step) for step in range(1, NX)]
    if ny > 1:
        partners += [at_y(1), at_y(-1)]
    partners += [sibling]
    barrier = pltpu.get_barrier_semaphore()
    for partner in partners:
        pl.semaphore_signal(barrier, inc=1, device_id=partner, device_id_type=MESH)

    for k in range(KV):
        q_ref[k] = q_in[:, :, k].reshape(ROWS, HEAD)

    lane1 = iota((1, ROWS), 1)
    stored = [om_ref[0, bl_ref[p % 2, p // 2]] for p in range(2 * REQ)]
    owner = [s // 2 for s in stored]
    code_rows = [jnp.zeros((1, ROWS), jnp.int32), jnp.zeros((1, ROWS), jnp.int32)]
    for p in range(2 * REQ):
        rank = jnp.int32(0)
        for other in range(p):
            rank = rank + (owner[other] == owner[p]).astype(jnp.int32)
        code = owner[p] * 4 + rank * 2 + stored[p] % 2
        code_rows[p % 2] = jnp.where(lane1 // 16 == p // 2, code, code_rows[p % 2])
    metaz[0, pl.ds(0, 1), :] = code_rows[0]
    metaz[0, pl.ds(1, 1), :] = code_rows[1]

    pl.semaphore_wait(barrier, len(partners))

    def q_half(b, h):
        rows = pl.ds(h * HALF, HALF)
        return q_ref.at[rows] if b == 0 else zq.at[b, rows]

    def pass_queries(b, h, step, into):
        send(
            q_half(b, h),
            zq.at[into, pl.ds(h * HALF, HALF)],
            sent_sem.at[0],
            zr_sem.at[into, h],
            at_z(step),
        )

    def forward_queries(b, h):
        for step in (1, -1):
            if b == 0 or (step == 1) == (b > zh):
                if b == zh:
                    continue
                into = (b - step) % nz
                if into == zh and h != (0 if step == 1 else 1):
                    continue
                pass_queries(b, h, step, into)

    def query_arrived(b, h):
        arrived(zq.at[b, pl.ds(h * HALF, HALF)], zr_sem.at[b, h])

    for step in range(1, nz):
        send(
            metaz.at[0],
            metaz.at[(-step) % nz],
            sent_sem.at[1],
            all_sem.at[0],
            at_z(step),
        )

    for h in range(2):
        forward_queries(0, h)

    loads[0].wait()
    loads[1].wait()

    def share_root(b):
        send(rkv.at[b], rkv.at[ny + b], sent_sem.at[2], all_sem.at[1], sibling)

    def forward_root(b):
        for step in (1, -1):
            if b == 0 or (step == 1) == (b > yh):
                if b == yh or ny == 1:
                    continue
                into = (b - step) % ny
                if into == yh:
                    part = 0 if step == 1 else 1
                    send(
                        rkv.at[b, part],
                        rkv.at[into, part],
                        sent_sem.at[3],
                        yr_sem.at[into, part],
                        at_y(step),
                    )
                else:
                    send(
                        rkv.at[b],
                        rkv.at[into],
                        sent_sem.at[3],
                        yr_sem.at[into, 0],
                        at_y(step),
                    )

    def root_arrived(b):
        if b == yh:
            for part in range(2):
                arrived(rkv.at[b, part], yr_sem.at[b, part])
        else:
            arrived(rkv.at[b], yr_sem.at[b, 0])

    forward_root(0)
    share_root(0)

    row = iota((ROWS, ROWS), 0)
    lane = iota((ROWS, ROWS), 1)
    same_place = row % 16 == lane % 16
    diagonal = jnp.where(row == lane, 0.0, DROP)

    def there(step):
        return pl.ds(pl.multiple_of(lax.rem(x + step, NX) * SLOT_ROWS, SLOT_ROWS), SLOT_ROWS)

    mine = there(0)
    others = pl.ds(0, (NX - 1) * SLOT_ROWS)

    def route(b):
        wanted = z * (2 * NX) + row // 16
        first = metaz[b, pl.ds(0, 1), :] // 2
        second = metaz[b, pl.ds(1, 1), :] // 2
        hit = ((first == wanted) | (second == wanted)) & same_place
        onehot[b] = jnp.where(hit, 1.0, 0.0).astype(jnp.bfloat16)
        bias_t[b] = jnp.where(hit, 0.0, DROP).T

    def select(b, h):
        part = pl.ds(h * HALF, HALF)

        def body(k, carry):
            block = q_ref[k] if b == 0 else zq[b, k]
            chosen = jnp.dot(onehot[b], block, preferred_element_type=jnp.float32)
            snd[b, k] = chosen.astype(jnp.bfloat16)
            return carry

        lax.fori_loop(h * HALF, (h + 1) * HALF, body, 0, unroll=True)
        for step in range(1, NX):
            send(
                snd.at[b, part, there(step), :],
                rcv.at[b, part, mine, :],
                sent_sem.at[4],
                xr_sem.at[b, h],
                at_x(step),
            )

        def keep(k, carry):
            rcv[b, k, mine, :] = snd[b, k, mine, :]
            return carry

        lax.fori_loop(h * HALF, (h + 1) * HALF, keep, 0, unroll=True)

    def slots_arrived(b, h):
        arrived(rcv.at[b, pl.ds(h * HALF, HALF), others, :], xr_sem.at[b, h])

    ones_prefix = jnp.ones((BLK, HEAD), jnp.bfloat16)

    def label_slots(b):
        for source in range(NX):
            code = metax[source, b]
            srow = iota((SLOT_ROWS, ROWS), 0)
            slane = iota((SLOT_ROWS, ROWS), 1)
            wanted = (dev * 2 + srow // 16) * 2 + 1
            hit = (code[0:1, :] == wanted) | (code[1:2, :] == wanted)
            second = jnp.max(jnp.where(hit, 1.0, 0.0), axis=1, keepdims=True)
            here = pl.ds(source * SLOT_ROWS, SLOT_ROWS)
            pick[b, here, :] = jnp.where(
                slane == 0, 1.0 - second, jnp.where(slane == 1, second, 0.0)
            ).astype(jnp.bfloat16)
            second_slot[b, here, :] = jnp.broadcast_to(second, (SLOT_ROWS, ROWS))

    def serve(blocks, halves):
        rows = len(blocks) * ROWS
        last = HALF * (halves[-1] + 1) - 1

        def score(k, into):
            cols = pl.ds(pl.multiple_of(k * HEAD, HEAD), HEAD)
            queries = jnp.concatenate(
                [jnp.concatenate([rcv[b, k], pick[b]], axis=1) for b in blocks], axis=0
            )
            keys = jnp.concatenate([pk[:, cols], kbias[...]], axis=1)
            both = lax.dot_general(queries, keys, NT, preferred_element_type=jnp.float32)
            into[pl.ds(0, rows), :] = jnp.maximum(both[:, :BLK], both[:, BLK:])

        def weigh(k, source):
            cols = pl.ds(pl.multiple_of(k * HEAD, HEAD), HEAD)
            scores = source[pl.ds(0, rows), :]
            highest = jnp.max(scores, axis=1, keepdims=True)
            weights = jnp.exp2((scores - highest) * SCALE2).astype(jnp.bfloat16)
            values = jnp.concatenate([pv[:BLK, cols], pv[BLK:, cols], ones_prefix], axis=1)
            summed = jnp.dot(weights, values, preferred_element_type=jnp.float32)
            totals = summed[:, 2 * HEAD :]
            inverse = 1.0 / totals
            logs = highest * SCALE2 + jnp.log(totals) * LOG2E
            for at, b in enumerate(blocks):
                part = slice(at * ROWS, (at + 1) * ROWS)
                chosen = jnp.where(
                    second_slot[b] > 0.5, summed[part, HEAD : 2 * HEAD], summed[part, :HEAD]
                )
                ans[b, k] = (chosen * inverse[part]).astype(jnp.bfloat16)
                lacc[at] = jnp.where(lane == k, logs[part], lacc[at])

        def body(turn, carry):
            k = HALF * halves[0] + 2 * turn
            score(k + 1, score_odd)
            weigh(k, score_even)
            score(jnp.minimum(k + 2, last), score_even)
            weigh(k + 1, score_odd)
            return carry

        score(HALF * halves[0], score_even)
        lax.fori_loop(0, len(halves) * HALF // 2, body, 0)
        for at, b in enumerate(blocks):
            logs = lacc[at].T[:KV, :]
            for h in halves:
                lmine[b, h] = logs

    def give_back(b, h):
        part = pl.ds(h * HALF, HALF)
        for step in range(1, NX):
            send(
                ans.at[b, part, there(step), :],
                ret.at[b, part, mine, :],
                sent_sem.at[5],
                br_sem.at[b, h],
                at_x(step),
            )
            send(
                lmine.at[b, h],
                lret.at[b, h, NX - step],
                sent_sem.at[6],
                lr_sem.at[b, h],
                at_x(step),
            )

        def body(k, carry):
            ret[b, k, mine, :] = ans[b, k, mine, :]
            return carry

        lax.fori_loop(h * HALF, (h + 1) * HALF, body, 0, unroll=True)

    def answers_arrived(b, h):
        lane8 = iota((KV, ROWS), 1)
        rows = lmine[b, h]
        arrived(ret.at[b, pl.ds(h * HALF, HALF), others, :], br_sem.at[b, h])
        arrived(lret.at[b, h, pl.ds(1, NX - 1)], lr_sem.at[b, h])
        for step in range(1, NX):
            moved = pltpu.roll(lret[b, h, step], SLOT_ROWS * step, 1)
            rows = jnp.where(lane8 // SLOT_ROWS == lax.rem(x + step, NX), moved, rows)
        lslot[b, h] = rows

    def chain(b, h):
        step = 1 if b < zh or (b == zh and h == 0) else -1
        into = (b - step) % nz
        place = into if into else (0 if step == 1 else zh)
        return step, place

    def has_input(b, h):
        return b != zh and (b not in (zh - 1, zh + 1) or chain(zh, h)[1] == b)

    def partial_arrived(place, h):
        arrived(rsin.at[place, pl.ds(h * HALF, HALF)], rr_sem.at[place, h])
        arrived(lin.at[place, h], er_sem.at[place, h])

    def combine(blocks, h):
        for b in blocks:
            if has_input(b, h):
                partial_arrived(b, h)

        def body(k, carry):
            def logs(b):
                rows = jnp.broadcast_to(lslot[b, h, pl.ds(k, 1), :], (ROWS, ROWS)) + bias_t[b]
                if has_input(b, h):
                    extra = jnp.broadcast_to(lin[b, h, pl.ds(k, 1), :], (ROWS, ROWS)) + diagonal
                    rows = jnp.concatenate([rows, extra], axis=1)
                return rows

            highest = [
                jnp.maximum(jnp.max(logs(b), axis=1, keepdims=True), FLOOR) for b in blocks
            ]
            weights = [jnp.exp2(logs(b) - top).astype(jnp.bfloat16) for b, top in zip(blocks, highest)]
            sums = []
            for b, weight in zip(blocks, weights):
                parts = ret[b, k]
                if has_input(b, h):
                    parts = jnp.concatenate([parts, rsin[b, k]], axis=0)
                parts = jnp.concatenate([parts, jnp.ones_like(parts)], axis=1)
                sums.append(jnp.dot(weight, parts, preferred_element_type=jnp.float32))
            for at, b in enumerate(blocks):
                totals = jnp.maximum(sums[at][:, HEAD:], 1.0e-30)
                rsout[b, k] = (sums[at][:, :HEAD] / totals).astype(jnp.bfloat16)
                lacc[at] = jnp.where(lane == k, highest[at] + jnp.log(totals) * LOG2E, lacc[at])
            return carry

        lax.fori_loop(h * HALF, (h + 1) * HALF, body, 0, unroll=2)
        for at, b in enumerate(blocks):
            lout[b, h] = lacc[at].T[:KV, :]
            step, place = chain(b, h)
            part = pl.ds(h * HALF, HALF)
            send(
                rsout.at[b, part],
                rsin.at[place, part],
                sent_sem.at[7],
                rr_sem.at[place, h],
                at_z(step),
            )
            send(
                lout.at[b, h],
                lin.at[place, h],
                sent_sem.at[8],
                er_sem.at[place, h],
                at_z(step),
            )

    ones_root = jnp.ones((ny * CORES * rkv.shape[2], HEAD), jnp.bfloat16)
    ones_local = jnp.ones((LOCAL, HEAD), jnp.bfloat16)
    root_rows = ny * CORES * rkv.shape[2]

    def attend_local(k_from, k_to):
        def body(k, carry):
            cols = pl.ds(pl.multiple_of(k * HEAD, HEAD), HEAD)
            queries = q_ref[k]
            root_keys = rkv[:, 0, :, cols].reshape(root_rows, HEAD)
            root_values = rkv[:, 1, :, cols].reshape(root_rows, HEAD)
            root_scores = lax.dot_general(
                queries, root_keys, NT, preferred_element_type=jnp.float32
            )
            wide = jnp.concatenate([queries, lpick[...]], axis=1)
            keys = jnp.concatenate([sk[:, cols], lbias[...]], axis=1)
            scores = lax.dot_general(wide, keys, NT, preferred_element_type=jnp.float32)
            highest = jnp.maximum(
                jnp.max(root_scores, axis=1, keepdims=True),
                jnp.max(scores, axis=1, keepdims=True),
            )
            root_weights = jnp.exp2((root_scores - highest) * SCALE2).astype(jnp.bfloat16)
            weights = jnp.exp2((scores - highest) * SCALE2).astype(jnp.bfloat16)
            summed = jnp.dot(
                root_weights,
                jnp.concatenate([root_values, ones_root], axis=1),
                preferred_element_type=jnp.float32,
            ) + jnp.dot(
                weights,
                jnp.concatenate([sv[:, cols], ones_local], axis=1),
                preferred_element_type=jnp.float32,
            )
            loc_acc[k] = summed[:, :HEAD]
            loc_tot[k] = summed[:, HEAD:]
            loc_max[k] = jnp.broadcast_to(highest * SCALE2, (ROWS, ROWS))
            return carry

        lax.fori_loop(k_from, k_to, body, 0)

    def finish(h):
        partial_arrived(0, h)
        partial_arrived(zh, h)

        def body(k, carry):
            rows = jnp.concatenate(
                [
                    jnp.broadcast_to(lslot[0, h, pl.ds(k, 1), :], (ROWS, ROWS)) + bias_t[0],
                    jnp.broadcast_to(lin[0, h, pl.ds(k, 1), :], (ROWS, ROWS)) + diagonal,
                    jnp.broadcast_to(lin[zh, h, pl.ds(k, 1), :], (ROWS, ROWS)) + diagonal,
                ],
                axis=1,
            )
            highest = jnp.maximum(jnp.max(rows, axis=1, keepdims=True), loc_max[k])
            wide = jnp.concatenate([highest] * 3, axis=1)
            weights = jnp.exp2(rows - wide).astype(jnp.bfloat16)
            parts = jnp.concatenate([ret[0, k], rsin[0, k], rsin[zh, k]], axis=0)
            parts = jnp.concatenate([parts, jnp.ones_like(parts)], axis=1)
            summed = jnp.dot(weights, parts, preferred_element_type=jnp.float32)
            share = jnp.exp2(loc_max[k] - highest)
            numerator = summed[:, :HEAD] + loc_acc[k] * share
            denominator = summed[:, HEAD:] + loc_tot[k] * share
            out_ref[:, :, k] = (
                (numerator / denominator).astype(jnp.bfloat16).reshape(REQ, 2, KV, HEAD)
            )
            return carry

        lax.fori_loop(h * HALF, (h + 1) * HALF, body, 0, unroll=2)

    lacc[...] = jnp.zeros_like(lacc)
    route(0)
    for h in range(2):
        select(0, h)

    prow = iota((2 * BLK, HEAD), 0)
    plane = iota((2 * BLK, HEAD), 1)
    limit = jnp.where(prow < BLK, plen_ref[0], plen_ref[1])
    live = prow % BLK < limit
    kbias[...] = jnp.where(
        (plane < 2) & ~((plane == prow // BLK) & live), DROP, 0.0
    ).astype(jnp.bfloat16)
    lrow = iota((LOCAL, HEAD), 0)
    llane = iota((LOCAL, HEAD), 1)
    length = jnp.zeros((LOCAL, HEAD), jnp.int32)
    for r in range(REQ):
        length = jnp.where(lrow // SUF == r, slen_ref[r], length)
    past = (lrow < REQ * SUF) & (llane // 2 == lrow // SUF) & (lrow % SUF < length)
    fresh_row = lrow - REQ * SUF
    fresh = (
        (fresh_row >= 0) & (llane // 2 == fresh_row // 16) & (fresh_row % 16 <= llane % 2)
    )
    lbias[...] = jnp.where((llane < 2 * REQ) & ~(past | fresh), DROP, 0.0).astype(jnp.bfloat16)
    lpick[...] = jnp.where(lane == row // 8, 1.0, 0.0).astype(jnp.bfloat16)
    for cache, new in ((sk, nk_ref), (sv, nv_ref)):
        cache[pl.ds(REQ * SUF, 16 * REQ), :] = jnp.zeros((16 * REQ, KV * HEAD), jnp.bfloat16)
        for r in range(REQ):
            cache[pl.ds(REQ * SUF + 16 * r, 2), :] = new[r]

    for load in loads[2:]:
        load.wait()
    def exchange_routes():
        arrived(metaz.at[pl.ds(1, nz - 1)], all_sem.at[0])
        for step in range(1, NX):
            send(
                metaz,
                metax.at[x],
                sent_sem.at[9],
                all_sem.at[2],
                at_x(step),
            )
        metax[x] = metaz[...]

    def advance_root(s):
        for b in (ny - s, s) if s < yh else (yh,):
            root_arrived(b)
            forward_root(b)
            share_root(b)

    def serve_step(s):
        blocks = (nz - s, s) if 0 < s < zh else (s,)
        for b in blocks:
            label_slots(b)
            for h in range(2):
                slots_arrived(b, h)
        serve(blocks, (0, 1))

    served = 0
    for s in range(1, zh + 1):
        blocks = (nz - s, s) if s < zh else (zh,)
        for h in range(2):
            for b in blocks:
                query_arrived(b, h)
                forward_queries(b, h)
        if s == 1:
            exchange_routes()
        for b in blocks:
            route(b)
        for h in range(2):
            for b in blocks:
                select(b, h)
        if s == min(2, zh):
            arrived(metax.at[pl.ds(0, NX - 1)], all_sem.at[2])
        while served < s - 1:
            serve_step(served)
            served += 1
        if s < min(zh, yh):
            advance_root(s)
        if s == zh - 1 and s > 1:
            serve_step(served)
            served += 1
    while served < zh:
        serve_step(served)
        served += 1
    label_slots(zh)

    order = [(zh,)] + [(s, nz - s) for s in range(zh - 1, 0, -1)] + [(0,)]
    for h in range(2):
        slots_arrived(zh, h)
        serve((zh,), (h,))
        give_back(zh, h)

    for s in range(min(zh, yh), yh + 1):
        advance_root(s)
    shares = [-(-KV * turn // (zh - 1)) for turn in range(zh)]
    for b in order[1]:
        give_back(b, 0)
    for turn, blocks in enumerate(order[:-1]):
        for h in range(2):
            for b in blocks:
                answers_arrived(b, h)
            if turn == 0:
                ahead = [(b, 1) for b in order[1]] if h == 0 else []
            else:
                ahead = [(b, h) for b in order[turn + 1]]
            for b, part in ahead:
                give_back(b, part)
            combine(blocks, h)
        if turn == 0:
            arrived(rkv.at[pl.ds(ny, ny)], all_sem.at[1])
        else:
            attend_local(shares[turn - 1], shares[turn])
    for h in range(2):
        answers_arrived(0, h)
        finish(h)

    for at, ref in enumerate(
        (
            zq.at[pl.ds(1, nz - 1)],
            metaz.at[pl.ds(1, nz - 1)],
            rkv.at[pl.ds(0, ny)],
            rkv.at[pl.ds(1, ny - 1)],
            rcv.at[:, :, others, :],
            ret.at[:, :, others, :],
            lret.at[:, :, pl.ds(1, NX - 1)],
            rsin.at[pl.ds(1, nz - 1)],
            lin.at[pl.ds(1, nz - 1)],
            metax.at[pl.ds(1, NX - 1)],
        )
    ):
        arrived(ref, sent_sem.at[at])


def shards(nz, ny, *args):
    (
        queries,
        new_keys,
        new_values,
        suffix_keys,
        suffix_values,
        suffix_lengths,
        root_keys,
        root_values,
        prefix_keys,
        prefix_values,
        prefix_lengths,
        owner_map,
        block_lists,
    ) = args
    width = KV * HEAD
    root_rows = root_keys.shape[0]
    bf16, f32 = jnp.bfloat16, jnp.float32
    vmem = pl.BlockSpec(memory_space=pltpu.VMEM)
    smem = pl.BlockSpec(memory_space=pltpu.SMEM)
    anywhere = pl.BlockSpec(memory_space=pl.ANY)
    dma = pltpu.SemaphoreType.DMA
    blocks = (nz, KV, ROWS, HEAD)
    out = pl.pallas_call(
        functools.partial(kernel, nz, ny),
        out_shape=jax.ShapeDtypeStruct((REQ, 2, KV, 8, HEAD), bf16),
        in_specs=[vmem, vmem, vmem] + [anywhere] * 6 + [smem] * 4,
        out_specs=vmem,
        scratch_shapes=[
            pltpu.VMEM(blocks[1:], bf16),
            pltpu.VMEM(blocks, bf16),
            pltpu.VMEM(blocks, bf16),
            pltpu.VMEM(blocks, bf16),
            pltpu.VMEM(blocks, bf16),
            pltpu.VMEM(blocks, bf16),
            pltpu.VMEM(blocks, bf16),
            pltpu.VMEM(blocks, bf16),
            pltpu.VMEM((2 * ny, 2, root_rows, width), bf16),
            pltpu.VMEM((2 * BLK, width), bf16),
            pltpu.VMEM((2 * BLK, width), bf16),
            pltpu.VMEM((LOCAL, width), bf16),
            pltpu.VMEM((LOCAL, width), bf16),
            pltpu.VMEM((nz, 2, ROWS), jnp.int32),
            pltpu.VMEM((NX, nz, 2, ROWS), jnp.int32),
            pltpu.VMEM((nz, ROWS, ROWS), bf16),
            pltpu.VMEM((nz, ROWS, ROWS), f32),
            pltpu.VMEM((nz, ROWS, HEAD), bf16),
            pltpu.VMEM((2 * BLK, HEAD), bf16),
            pltpu.VMEM((LOCAL, HEAD), bf16),
            pltpu.VMEM((ROWS, HEAD), bf16),
            pltpu.VMEM((nz, 2, KV, ROWS), f32),
            pltpu.VMEM((nz, 2, NX, KV, ROWS), f32),
            pltpu.VMEM((nz, 2, KV, ROWS), f32),
            pltpu.VMEM((nz, 2, KV, ROWS), f32),
            pltpu.VMEM((nz, 2, KV, ROWS), f32),
            pltpu.VMEM((KV, ROWS, HEAD), f32),
            pltpu.VMEM((KV, ROWS, HEAD), f32),
            pltpu.VMEM((KV, ROWS, HEAD), f32),
            pltpu.VMEM((2, ROWS, ROWS), f32),
            pltpu.VMEM((nz, ROWS, ROWS), f32),
            pltpu.VMEM((2 * ROWS, BLK), f32),
            pltpu.VMEM((2 * ROWS, BLK), f32),
            dma((6,)),
            dma((10,)),
            dma((3,)),
            dma((nz, 2)),
            dma((nz, 2)),
            dma((nz, 2)),
            dma((nz, 2)),
            dma((nz, 2)),
            dma((nz, 2)),
            dma((ny, 2)),
        ],
        compiler_params=pltpu.CompilerParams(
            collective_id=0, has_side_effects=True, vmem_limit_bytes=60 * 1024 * 1024 + 512 * 1024
        ),
        cost_estimate=pl.CostEstimate(
            flops=4_000_000_000, bytes_accessed=5_000_000, transcendentals=8_000_000
        ),
        name="shared_prefix_attention",
    )(
        queries.reshape(REQ, 2, KV, 8, HEAD),
        new_keys,
        new_values,
        suffix_keys.reshape(REQ * SUF, width),
        suffix_values.reshape(REQ * SUF, width),
        root_keys,
        root_values,
        prefix_keys.reshape(2 * BLK, width),
        prefix_values.reshape(2 * BLK, width),
        suffix_lengths,
        prefix_lengths,
        owner_map,
        block_lists.T,
    )
    return out.reshape(REQ, 2, 64 * HEAD)


def solution(mesh):
    return jax.shard_map(
        functools.partial(shards, mesh.shape["dev"] // NX, mesh.shape["group"] // CORES),
        mesh=mesh,
        in_specs=(
            P(("group", "dev"), None, None),
            P(("group", "dev"), None, None),
            P(("group", "dev"), None, None),
            P(("group", "dev"), None, None),
            P(("group", "dev"), None, None),
            P(("group", "dev")),
            P("group", None),
            P("group", None),
            P(("group", "dev"), None, None),
            P(("group", "dev"), None, None),
            P(("group", "dev")),
            P("group", None),
            P(("group", "dev"), None),
        ),
        out_specs=P(("group", "dev"), None, None),
        check_vma=False,
    )
```
